32 devices in a mesh: grp: 4 (over y, core), tp: 8 (over z, x).
Axes of the slice: x: 2, y: 2, z: 4, core: 2. Of those that a mesh axis runs over, the one named last changes fastest.
Arguments:
- queries: bfloat16 [4, 130, 8192], P('grp', None, 'tp'), may hold values from -24 to 24
- new_kv: bfloat16 [4, 128, 2048], P('grp', 'tp'), may hold values from -6 to 6
- decode_kv: bfloat16 [4, 2, 2048], P('grp'), may hold values from -6 to 6
- pool: bfloat16 [768, 16, 2048], P(('grp', 'tp')), may hold values from -12 to 12
- hist_pages: int32 [4], replicated, may hold values from 1 to 192, 384 in all
- owner: int32 [4], replicated, may hold values from 0 to 3, as said below
- block_table: int32 [4, 192], replicated, may hold values from 0 to 23, as said below
Outputs:
- attended: bfloat16 [4, 130, 8192], P('grp', None, 'tp')
- returned: bfloat16 [4, 128, 2048], P('grp', None, 'tp')
The draws below stay inside these ranges and needn't reach their ends.
Inputs may be any that keep to these rules, and one draw needn't show every extreme that they name: `hist_pages`: in every draw one session has exactly 192 pages, and the counts add up to 384. `owner`: each group owns exactly one session; in every draw some session s is owned by group (s + 2) mod 4. block_table[s, p] lies in [s * 6, (s + 1) * 6); the pages of one session on one device take distinct slots.
All inputs are finite; a program needn't handle non-finite values.
Results may differ from the reference program's by a relative error of at most 0.001.
Values may be sent and summed in bfloat16 or wider, within the bound.
No kernel may reach another device: no remote copies, remote signals or barrier semaphores. Data moves between devices by JAX's collectives and lax.ppermute only.
A program may use at most 320 MiB of HBM per device.

```python
import math
import jax
import jax.numpy as jnp
import numpy as np
from jax import lax

H = 64
KVH = 8
HD = 128
PAGE = 16
DEC = 2
NEW = 128
CAP = 6
S = 4
MAXP = 192
POOL = 24
POOL_ALL = 768
QROWS = 130
GROUP = 8
KVW = 2048
N_GRP = 4
N_TP = 8


def draw_queries(key, part):
    key = jax.random.fold_in(key, 5)
    shape = (S, QROWS, H * HD)
    base = jnp.clip(3.0 * jax.random.normal(key, shape, jnp.float32), -16.0, 16.0)
    return base.astype(jnp.bfloat16)


def draw_pool(key, part):
    key = jax.random.fold_in(key, 3)
    shape = (POOL_ALL, PAGE, KVW)
    base = jnp.clip(jax.random.normal(key, shape, jnp.float32), -6.0, 6.0)
    return base.astype(jnp.bfloat16)


def draw_owner(key, part):
    key = jax.random.fold_in(key, 9)
    order = jax.random.permutation(jax.random.fold_in(key, 1), N_GRP).astype(jnp.int32)
    target = jax.random.randint(jax.random.fold_in(key, 2), (), 0, N_GRP).astype(jnp.int32)
    holder = (target + N_GRP // 2) % N_GRP
    places = jnp.arange(N_GRP, dtype=jnp.int32)
    where_target = jnp.sum(jnp.where(order == target, places, 0)).astype(jnp.int32)
    displaced = order[holder]
    order = order.at[where_target].set(displaced)
    order = order.at[holder].set(target)
    return order.astype(jnp.int32)


def draw_block_table(key, part):
    key = jax.random.fold_in(key, 7)
    scores = jax.random.randint(key, (S, N_GRP, N_TP, CAP), 0, 1048576) * CAP + jnp.arange(CAP, dtype=jnp.int32)
    order = jnp.argsort(scores, axis=-1, stable=True).astype(jnp.int32)
    page_ids = jnp.arange(MAXP, dtype=jnp.int32)
    offset_of = page_ids // N_TP % N_GRP
    rank_of = page_ids % N_TP
    span_of = page_ids // (N_TP * N_GRP)
    sessions = jnp.arange(S, dtype=jnp.int32)[:, None]
    picked = order[sessions, offset_of[None, :], rank_of[None, :], span_of[None, :]]
    return (sessions * CAP + picked).astype(jnp.int32)


def shard_levels(stream_key, shape, shards, smallest, high):
    gain = 1.0
    for position, blocks in shards:
        draws = jax.random.uniform(jax.random.fold_in(jax.random.fold_in(stream_key, 6), position), (blocks,), jnp.float32, smallest / len(shards), high / len(shards))
        gain = gain * jnp.repeat(jnp.exp(draws), shape[position] // blocks).reshape((-1,) + (1,) * (len(shape) - 1 - position))
    return gain


def split_up(number_of, total, reach, lean):
    loads = [(1 << 20) // math.isqrt(grade ** lean) + 1 for grade in range(2, number_of + 1)]
    surplus, counts = total - reach - (number_of - 1), [1] * (number_of - 1)
    while surplus > 0:
        movable = [i for i in range(number_of - 1) if counts[i] < reach]
        whole, budget = sum([loads[i] for i in movable]), surplus
        for i in movable:
            addition = min(reach - counts[i], max(1, budget * loads[i] // whole), surplus)
            counts[i] = counts[i] + addition
            surplus = surplus - addition
    return np.array([reach] + counts)


def uneven(rng, count, total, bound, lean):
    if count == 2:
        one = jax.random.randint(rng, (), max(1, total - bound), min(bound, total - 1) + 1)
        return jnp.stack([one, total - one])
    lengths = jnp.asarray(split_up(count, total, bound, lean), jnp.int32)
    twos = (count - 1) // 2
    donor, sink = lengths[1:1 + 2 * twos:2], lengths[2:2 + 2 * twos:2]
    margin = jnp.minimum(donor - 1, bound - sink)
    moved = jax.random.randint(jax.random.fold_in(rng, 1), (twos,), 0, 1 << 20) % (margin + 1)
    lengths = lengths.at[1:1 + 2 * twos:2].set(donor - moved).at[2:2 + 2 * twos:2].set(sink + moved)
    return lengths[jax.random.permutation(jax.random.fold_in(rng, 2), count)]


def gaussian(key, dims, deviation, limit, shards=(), kind=jnp.bfloat16):
    array = jax.random.normal(key, dims, jnp.float32) * deviation
    if len(shards) > 0:
        array = shard_levels(key, dims, shards, -0.22, 0.18) * array
    return jnp.clip(array, min=-limit, max=limit).astype(kind)


def setup_inputs(seed: int = 0) -> dict:
    key_of = jax.random.split(jax.random.key(seed), 8)
    queries = draw_queries(jax.random.fold_in(key_of[7], 71), 0)
    new_kv = gaussian(key_of[1], (S, NEW, KVW), 1.0, 6.0, ((0, 4), (1, 8)))
    decode_kv = gaussian(key_of[2], (S, DEC, KVW), 1.0, 6.0, ((0, 4),))
    pool = draw_pool(jax.random.fold_in(key_of[7], 71), 0)
    hist_pages = uneven(key_of[4], S, S * MAXP // 2, MAXP, 2).astype(jnp.int32)
    owner = draw_owner(jax.random.fold_in(key_of[7], 71), 0)
    block_table = draw_block_table(jax.random.fold_in(key_of[7], 71), 0)
    return dict(queries=queries, new_kv=new_kv, decode_kv=decode_kv, pool=pool, hist_pages=hist_pages, owner=owner, block_table=block_table)


def head_attention(inputs):
    query, keys, values, visible = inputs
    score = jnp.einsum("rgd,kd->rgk", query.astype(jnp.float32), keys.astype(jnp.float32), precision=lax.Precision.HIGHEST) * (HD ** -0.5)
    score = jnp.where(visible[:, None, :], score, -jnp.inf)
    maximum = jnp.max(score, axis=2, keepdims=True)
    weight = jnp.exp(score - maximum)
    totals = jnp.sum(weight, axis=2, keepdims=True)
    mixed = jnp.einsum("rgk,kd->rgd", weight, values.astype(jnp.float32), precision=lax.Precision.HIGHEST)
    return mixed / totals


def reference(queries, new_kv, decode_kv, pool, hist_pages, owner, block_table):
    stacked = pool.reshape(N_GRP, N_TP, POOL, PAGE, KVW)
    page_ids = jnp.arange(MAXP, dtype=jnp.int32)

    def one_session(inputs):
        query, fresh_rows, decode_rows, pages_used, home, table = inputs
        group_of = (home + page_ids // N_TP) % N_GRP
        rank_of = page_ids % N_TP
        history = stacked[group_of, rank_of, table].reshape(MAXP * PAGE, KVW)
        all_rows = jnp.concatenate([history, fresh_rows, decode_rows], axis=0)
        count = all_rows.shape[0]
        key_index = jnp.arange(count, dtype=jnp.int32)
        query_index = jnp.arange(QROWS, dtype=jnp.int32)
        relative = key_index - MAXP * PAGE
        visible = jnp.where(key_index[None, :] < MAXP * PAGE, (key_index < pages_used * PAGE)[None, :], relative[None, :] <= query_index[:, None])
        split = all_rows.reshape(count, 2, KVH, HD)
        keys = jnp.transpose(split[:, 0], (1, 0, 2))
        values = jnp.transpose(split[:, 1], (1, 0, 2))
        heads = jnp.transpose(query.reshape(QROWS, KVH, GROUP, HD), (1, 0, 2, 3))
        visible_all = jnp.broadcast_to(visible[None], (KVH, QROWS, count))
        mixed = lax.map(head_attention, (heads, keys, values, visible_all))
        return jnp.transpose(mixed, (1, 0, 2, 3)).reshape(QROWS, H * HD).astype(jnp.bfloat16)

    attended = lax.map(one_session, (queries, new_kv, decode_kv, hist_pages, owner, block_table))
    returned = jnp.zeros((N_GRP, NEW, KVW), jnp.bfloat16).at[owner].set(new_kv)
    return attended, returned
```

```python
import functools
import math

import jax
import jax.numpy as jnp
from jax import lax
from jax.experimental import pallas as pl
from jax.experimental.pallas import tpu as pltpu
from jax.sharding import PartitionSpec as P

H = 64
KVH = 8
HD = 128
FLOOR = -1e30
ANY = pl.BlockSpec(memory_space=pl.ANY)
SMEM = pl.BlockSpec(memory_space=pltpu.SMEM)
VMEM = pl.BlockSpec(memory_space=pltpu.VMEM)
LIMIT = 56 * 1024 * 1024


def live_pages(session, group, rank, hist_ref, owner_ref, groups, ways):
    step = groups * ways
    first = lax.rem(group - owner_ref[session] + groups, groups) * ways + rank
    return lax.div(hist_ref[session] - first + step - 1, step)


def place(session, group, rank, hist_ref, owner_ref, groups, ways):
    def add(s, total):
        n = live_pages(s, group, rank, hist_ref, owner_ref, groups, ways)
        return total + jnp.where(s < session, n, 0)

    offset = lax.fori_loop(0, groups, add, jnp.int32(0), unroll=groups <= 4)
    return offset, live_pages(session, group, rank, hist_ref, owner_ref, groups, ways)


def pack_kernel(dims, hist_ref, owner_ref, table_ref, pool_ref, new_ref, *refs):
    groups, ways, capacity, packed, page, width = dims
    outs, stage, sem = refs[:ways], refs[ways], refs[ways + 1]
    group, rank = lax.axis_index("grp"), lax.axis_index("tp")
    stage[...] = jnp.zeros_like(stage)

    def each_session(s, at):
        first = lax.rem(group - owner_ref[s] + groups, groups) * ways + rank
        count = live_pages(s, group, rank, hist_ref, owner_ref, groups, ways)

        def each_page(j, at):
            slot = table_ref[s, j * groups * ways + first]
            pltpu.make_async_copy(pool_ref.at[slot], stage.at[at], sem.at[at]).start()
            return at + 1

        return lax.fori_loop(0, count, each_page, at)

    total = lax.fori_loop(0, groups, each_session, jnp.int32(0))
    repeat = ways // KVH

    def halves(shift):
        to = rank ^ shift
        key = pl.multiple_of(lax.div(to, repeat) * HD, HD)
        value = pl.multiple_of((KVH + lax.div(to, repeat)) * HD, HD)
        return to, key, value

    for shift in range(ways):
        to, key, value = halves(shift)
        outs[shift][packed, :, 0:HD] = new_ref[:, pl.ds(key, HD)]
        outs[shift][packed, :, HD:] = new_ref[:, pl.ds(value, HD)]
        columns = pl.multiple_of(to * width, width)
        outs[shift][packed + 1, :, 0:width] = new_ref[:, pl.ds(columns, width)]

    def drain(i, unused):
        pltpu.make_async_copy(pool_ref.at[0], stage.at[i], sem.at[i]).wait()
        return unused

    lax.fori_loop(0, total, drain, 0)

    for shift in range(ways):
        to, key, value = halves(shift)
        outs[shift][0:packed, :, 0:HD] = stage[:, :, pl.ds(key, HD)]
        outs[shift][0:packed, :, HD:] = stage[:, :, pl.ds(value, HD)]


def regroup_kernel(dims, shifts, hist_ref, owner_ref, *refs):
    groups, ways, capacity, packed = dims
    count = len(shifts)
    ins, outs = refs[:count], refs[count:]
    group, rank = lax.axis_index("grp"), lax.axis_index("tp")
    for i, shift in enumerate(shifts):
        for far in range(groups):
            offset, unused = place(group ^ far, group, rank ^ shift, hist_ref, owner_ref, groups, ways)
            start = jnp.minimum(offset, packed + 2 - capacity)
            outs[far][i, 0:capacity] = ins[i][pl.ds(start, capacity)]
            outs[far][i, capacity] = ins[i][packed + 1]


def attend_kernel(dims, refs, shifts, rounds):
    groups, ways, capacity, packed, page, rows, heads, local_new, decode = dims
    first, last = shifts == rounds[0], shifts == rounds[-1]
    hist_ref, owner_ref, query_ref = refs["hist"], refs["owner"], refs["query"]
    padded = -(-rows // 16) * 16
    group, rank = lax.axis_index("grp"), lax.axis_index("tp")
    stacked = refs["stacked"]

    copies, homeward = [], []
    if last:
        fresh = refs["fresh"]
        fresh[...] = jnp.zeros_like(fresh)
        for shift in range(ways):
            copies.append(pltpu.make_async_copy(
                refs["arrived"][shift].at[packed], fresh.at[rank ^ shift], refs["sems"].at[shift]))
        sender = jnp.int32(0)
        for s in range(groups):
            sender = sender + jnp.where(owner_ref[s] == group, s, 0)
        for far in range(groups):
            homeward.append((sender ^ group) == far)
            for part, sources in zip(refs["parts"], rounds):
                for i, shift in enumerate(sources):
                    copies.append((far, pltpu.make_async_copy(
                        part[far].at[i, capacity], refs["returned"].at[rank ^ shift],
                        refs["sems"].at[ways + shift])))
        for copy in copies[:ways]:
            copy.start()
        for far in range(groups):
            @pl.when(homeward[far])
            def start():
                for other, copy in copies[ways:]:
                    if other == far:
                        copy.start()

    for head in range(heads):
        stacked[head * padded:head * padded + rows, :] = query_ref[:, head * HD:(head + 1) * HD]
        stacked[head * padded + rows:(head + 1) * padded, :] = jnp.zeros((padded - rows, HD), jnp.bfloat16)

    keys = len(shifts) * capacity * page
    lane = lax.broadcasted_iota(jnp.int32, (1, keys), 1)
    masks = []
    for far in range(groups):
        seen = lane < 0
        for i, shift in enumerate(shifts):
            offset, live = place(group, group ^ far, rank ^ shift, hist_ref, owner_ref, groups, ways)
            low = (i * capacity + offset - jnp.minimum(offset, packed + 2 - capacity)) * page
            seen = seen | ((lane >= low) & (lane < low + live * page))
        masks.append(jnp.where(seen, 0.0, FLOOR).astype(jnp.float32))

    if last:
        for copy in copies[:ways]:
            copy.wait()
        fresh[ways, 0:page, 0:HD] = refs["decode"][:, pl.ds(pl.multiple_of(lax.div(rank, ways // KVH) * HD, HD), HD)]
        fresh[ways, 0:page, HD:] = refs["decode"][
            :, pl.ds(pl.multiple_of((KVH + lax.div(rank, ways // KVH)) * HD, HD), HD)]

    slope = HD ** -0.5 * math.log2(math.e)
    block_heads = min(heads, 4)
    tall = block_heads * padded

    def fold(state, query, key, value, bias):
        total, top, mixed = state
        score = lax.dot_general(query, key, (((1,), (1,)), ((), ())), preferred_element_type=jnp.float32) + bias
        new_top = jnp.maximum(top, jnp.max(score, axis=1, keepdims=True))
        weight = jnp.exp2((score - new_top) * slope)
        upper = weight.astype(jnp.bfloat16)
        lower = (weight - upper.astype(jnp.float32)).astype(jnp.bfloat16)
        wide = jnp.concatenate([value, jnp.ones_like(value)], axis=1)
        product = jnp.dot(upper, wide, preferred_element_type=jnp.float32)
        product = product + jnp.dot(lower, wide, preferred_element_type=jnp.float32)
        shrink = jnp.exp2((top - new_top) * slope)
        return total * shrink + product[:, HD:], new_top, mixed * shrink + product[:, :HD]

    for b in range(heads // block_heads):
        at = pl.ds(b * tall, tall)
        query = stacked[at, :]
        if first:
            state = (jnp.zeros((tall, HD), jnp.float32), jnp.full((tall, 1), FLOOR, jnp.float32),
                     jnp.zeros((tall, HD), jnp.float32))
        else:
            state = (refs["carry"][0][at, :], refs["carry"][1][at, :][:, :1], refs["carry"][2][at, :])
        for far in range(groups):
            block = refs["blocks"][far]
            rows_of = lambda low: jnp.concatenate(
                [block[i, 0:capacity, :, low:low + HD].reshape(capacity * page, HD) for i in range(len(shifts))], axis=0)
            state = fold(state, query, rows_of(0), rows_of(HD), masks[far])
        if last:
            units = fresh.shape[0]
            place_of = lax.broadcasted_iota(jnp.int32, (padded, units * page), 1)
            asker = lax.broadcasted_iota(jnp.int32, (padded, units * page), 0)
            unit, inside = lax.div(place_of, page), lax.rem(place_of, page)
            token = jnp.minimum(unit, ways) * local_new + inside
            real = ((unit < ways) & (inside < local_new)) | ((unit == ways) & (inside < decode))
            bias = jnp.where(real & (token <= asker), 0.0, FLOOR).astype(jnp.float32)
            bias = jnp.concatenate([bias] * block_heads, axis=0)
            state = fold(state, query, fresh[:, :, :HD].reshape(units * page, HD),
                         fresh[:, :, HD:].reshape(units * page, HD), bias)
            result = (state[2] / state[0]).astype(jnp.bfloat16)
            for h in range(block_heads):
                head = b * block_heads + h
                refs["out"][:, head * HD:(head + 1) * HD] = result[h * padded:h * padded + rows, :]
        else:
            refs["next"][0][at, :] = state[0]
            refs["next"][1][at, :] = jnp.broadcast_to(state[1], (tall, HD))
            refs["next"][2][at, :] = state[2]

    if last:
        for far in range(groups):
            @pl.when(homeward[far])
            def finish():
                for other, copy in copies[ways:]:
                    if other == far:
                        copy.wait()


def on_device(queries, new_kv, decode_kv, pool, hist_pages, owner, block_table):
    groups, ways = lax.axis_size("grp"), lax.axis_size("tp")
    slots, page, features = pool.shape
    capacity = slots // groups
    span = groups * ways
    rows = queries.shape[1]
    heads = H // ways
    local_new = new_kv.shape[1]
    decode = decode_kv.shape[1]
    width = features // ways
    pages_in_all = groups * block_table.shape[1] // 2
    packed = min(slots, (pages_in_all + groups * (span - 1) - ways * groups * (groups - 1) // 2) // span)
    rounds = [list(range(ways))]
    params = pltpu.CompilerParams(vmem_limit_bytes=LIMIT)

    new_rows = new_kv[0]
    if local_new < page:
        new_rows = jnp.pad(new_rows, ((0, page - local_new), (0, 0)))
    decode_rows = jnp.pad(decode_kv[0], ((0, page - decode), (0, 0)))

    unit = (page, 2 * HD)
    cut = pl.pallas_call(
        functools.partial(pack_kernel, (groups, ways, capacity, packed, page, width)),
        out_shape=[jax.ShapeDtypeStruct((packed + 2,) + unit, jnp.bfloat16)] * ways,
        in_specs=[SMEM, SMEM, SMEM, ANY, VMEM],
        out_specs=[VMEM] * ways,
        scratch_shapes=[pltpu.VMEM((packed, page, features), jnp.bfloat16), pltpu.SemaphoreType.DMA((packed,))],
        compiler_params=params,
    )(hist_pages, owner, block_table, pool, new_rows)
    arrived = [cut[0]] + [
        lax.ppermute(cut[shift], "tp", [(i, i ^ shift) for i in range(ways)]) for shift in range(1, ways)]

    parts, carry = [], None
    for shifts in rounds:
        sent = pl.pallas_call(
            functools.partial(regroup_kernel, (groups, ways, capacity, packed), shifts),
            out_shape=[jax.ShapeDtypeStruct((len(shifts), capacity + 1) + unit, jnp.bfloat16)] * groups,
            in_specs=[SMEM, SMEM] + [VMEM] * len(shifts),
            out_specs=[VMEM] * groups,
            compiler_params=params,
        )(hist_pages, owner, *[arrived[shift] for shift in shifts])
        parts.append([sent[0]] + [
            lax.ppermute(sent[far], "grp", [(i, i ^ far) for i in range(groups)]) for far in range(1, groups)])

    tall = heads * (-(-rows // 16) * 16)
    for shifts, blocks in zip(rounds, parts):
        last = shifts == rounds[-1]
        args = dict(hist=hist_pages, owner=owner, query=queries[0], blocks=blocks)
        specs = dict(hist=SMEM, owner=SMEM, query=VMEM, blocks=[VMEM] * groups)
        if carry is not None:
            args["carry"], specs["carry"] = list(carry), [VMEM] * 3
        scratch = dict(stacked=pltpu.VMEM((tall, HD), jnp.bfloat16))
        if last:
            args.update(arrived=arrived, decode=decode_rows, parts=parts)
            specs.update(arrived=[ANY] * ways, decode=VMEM, parts=[[ANY] * groups for unused in rounds])
            outs = dict(out=jax.ShapeDtypeStruct((rows, heads * HD), jnp.bfloat16),
                        returned=jax.ShapeDtypeStruct((ways,) + unit, jnp.bfloat16))
            out_specs = dict(out=VMEM, returned=ANY)
            scratch["fresh"] = pltpu.VMEM((-(-(ways + 1) // 8) * 8,) + unit, jnp.bfloat16)
            scratch["sems"] = pltpu.SemaphoreType.DMA((2 * ways,))
        else:
            outs = dict(next=[jax.ShapeDtypeStruct((tall, HD), jnp.float32)] * 3)
            out_specs = dict(next=[VMEM] * 3)
        flat_args, in_tree = jax.tree.flatten(args)
        flat_outs, out_tree = jax.tree.flatten(outs)
        flat_scratch, scratch_tree = jax.tree.flatten(scratch)

        def kernel(*flat, in_tree=in_tree, out_tree=out_tree, scratch_tree=scratch_tree, shifts=shifts):
            n, m = in_tree.num_leaves, out_tree.num_leaves
            refs = dict(jax.tree.unflatten(in_tree, flat[:n]))
            refs.update(jax.tree.unflatten(out_tree, flat[n:n + m]))
            refs.update(jax.tree.unflatten(scratch_tree, flat[n + m:]))
            dims = (groups, ways, capacity, packed, page, rows, heads, local_new, decode)
            attend_kernel(dims, refs, shifts, rounds)

        flat = pl.pallas_call(
            kernel,
            out_shape=flat_outs,
            in_specs=jax.tree.leaves(specs),
            out_specs=jax.tree.leaves(out_specs),
            scratch_shapes=flat_scratch,
            compiler_params=params,
        )(*flat_args)
        result = jax.tree.unflatten(out_tree, flat)
        carry = None if last else result["next"]
    returned = result["returned"][:, :local_new, :width].reshape(1, ways * local_new, width)
    return result["out"][None], returned


def solution(mesh):
    return jax.shard_map(
        on_device,
        mesh=mesh,
        in_specs=(
            P("grp", None, "tp"),
            P("grp", "tp", None),
            P("grp", None, None),
            P(("grp", "tp"), None, None),
            P(),
            P(),
            P(),
        ),
        out_specs=(P("grp", None, "tp"), P("grp", None, "tp")),
        check_vma=False,
    )
```

```python
import functools
import math

import jax
import jax.numpy as jnp
from jax import lax
from jax.experimental import pallas as pl
from jax.experimental.pallas import tpu as pltpu
from jax.sharding import PartitionSpec as P

H = 64
KVH = 8
HD = 128
FLOOR = -1e30
ANY = pl.BlockSpec(memory_space=pl.ANY)
SMEM = pl.BlockSpec(memory_space=pltpu.SMEM)
VMEM = pl.BlockSpec(memory_space=pltpu.VMEM)
LIMIT = 56 * 1024 * 1024


def divide(value, by):
    if by & (by - 1):
        return lax.div(value, by)
    return lax.shift_right_logical(value, by.bit_length() - 1)


def remainder(value, by):
    if by & (by - 1):
        return lax.rem(value, by)
    return value & (by - 1)


def live_pages(session, group, rank, hist_ref, owner_ref, groups, ways):
    step = groups * ways
    first = remainder(group - owner_ref[session] + groups, groups) * ways + rank
    return divide(hist_ref[session] - first + step - 1, step)


def place(session, group, rank, hist_ref, owner_ref, groups, ways):
    def add(s, total):
        n = live_pages(s, group, rank, hist_ref, owner_ref, groups, ways)
        return total + jnp.where(s < session, n, 0)

    offset = lax.fori_loop(0, groups, add, jnp.int32(0), unroll=groups <= 4)
    return offset, live_pages(session, group, rank, hist_ref, owner_ref, groups, ways)


def pack_kernel(dims, hist_ref, owner_ref, table_ref, pool_ref, new_ref, *refs):
    groups, ways, capacity, packed, page, width = dims
    outs, stage, sem = refs[:ways], refs[ways], refs[ways + 1]
    group, rank = lax.axis_index("grp"), lax.axis_index("tp")
    def each_session(s, at):
        first = remainder(group - owner_ref[s] + groups, groups) * ways + rank
        count = live_pages(s, group, rank, hist_ref, owner_ref, groups, ways)

        def each_page(j, at):
            slot = table_ref[s, j * groups * ways + first]
            pltpu.make_async_copy(pool_ref.at[slot], stage.at[at], sem.at[at]).start()
            return at + 1

        return lax.fori_loop(0, count, each_page, at)

    total = lax.fori_loop(0, groups, each_session, jnp.int32(0))
    repeat = ways // KVH

    def halves(shift):
        to = rank ^ shift
        key = pl.multiple_of(lax.div(to, repeat) * HD, HD)
        value = pl.multiple_of((KVH + lax.div(to, repeat)) * HD, HD)
        return to, key, value

    for shift in range(ways):
        to, key, value = halves(shift)
        outs[shift][packed, :, 0:HD] = new_ref[:, pl.ds(key, HD)]
        outs[shift][packed, :, HD:] = new_ref[:, pl.ds(value, HD)]
        columns = pl.multiple_of(to * width, width)
        outs[shift][packed + 1, :, 0:width] = new_ref[:, pl.ds(columns, width)]

    def blank(i, unused):
        stage[i] = jnp.zeros(stage.shape[1:], stage.dtype)
        return unused

    lax.fori_loop(total, packed, blank, 0)

    def drain(i, unused):
        pltpu.make_async_copy(pool_ref.at[0], stage.at[i], sem.at[i]).wait()
        return unused

    lax.fori_loop(0, total, drain, 0)

    for shift in range(ways):
        to, key, value = halves(shift)
        outs[shift][0:packed, :, 0:HD] = stage[:, :, pl.ds(key, HD)]
        outs[shift][0:packed, :, HD:] = stage[:, :, pl.ds(value, HD)]


def regroup_kernel(dims, shifts, hist_ref, owner_ref, *refs):
    groups, ways, capacity, packed = dims
    count = len(shifts)
    ins, outs, fresh = refs[:count], refs[-groups - 1:-1], refs[-1]
    group, rank = lax.axis_index("grp"), lax.axis_index("tp")
    for i, shift in enumerate(shifts):
        for far in range(groups):
            offset, unused = place(group ^ far, group, rank ^ shift, hist_ref, owner_ref, groups, ways)
            start = jnp.minimum(offset, packed + 2 - capacity)
            outs[far][i, 0:capacity] = ins[i][pl.ds(start, capacity)]
            outs[far][i, capacity] = ins[i][packed + 1]
        fresh[i] = ins[i][packed]


def attend_kernel(dims, refs, rounds, stages, number):
    groups, ways, capacity, packed, page, rows, heads, local_new, decode = dims
    first, last = number == 0, number == len(stages) - 1
    fresh_round = 0 if first else 1 if last else None
    hist_ref, owner_ref, query_ref = refs["hist"], refs["owner"], refs["query"]
    padded = -(-rows // 16) * 16
    group, rank = lax.axis_index("grp"), lax.axis_index("tp")
    stacked = refs["stacked"]

    homeward = []
    if last:
        sender = jnp.int32(0)
        for s in range(groups):
            sender = sender + jnp.where(owner_ref[s] == group, s, 0)
        for far in range(groups):
            home = [pltpu.make_async_copy(
                refs["parts"][r][far].at[i, capacity], refs["returned"].at[rank ^ shift], refs["home"].at[shift])
                for r, sources in enumerate(rounds) for i, shift in enumerate(sources)]
            homeward.append(((sender ^ group) == far, home))

            @pl.when(homeward[far][0])
            def start():
                for copy in homeward[far][1]:
                    copy.start()

    for head in range(heads):
        stacked[head * padded:head * padded + rows, :] = query_ref[:, head * HD:(head + 1) * HD]
        stacked[head * padded + rows:(head + 1) * padded, :] = jnp.zeros((padded - rows, HD), jnp.bfloat16)

    items = [(r, far, i) for r, far in stages[number] for i in range(len(rounds[r]))]
    many = -(-len(items) // -(-len(items) // 12))
    many = -(-many // 4) * 4
    chunks = [items[k:k + many] for k in range(0, len(items), many)]
    masks = []
    for chunk in chunks:
        lane = lax.broadcasted_iota(jnp.int32, (1, len(chunk) * capacity * page), 1)
        seen = lane < 0
        for n, (r, far, i) in enumerate(chunk):
            offset, live = place(group, group ^ far, rank ^ rounds[r][i], hist_ref, owner_ref, groups, ways)
            low = (n * capacity + offset - jnp.minimum(offset, packed + 2 - capacity)) * page
            seen = seen | ((lane >= low) & (lane < low + live * page))
        masks.append(jnp.where(seen, 0.0, FLOOR).astype(jnp.float32))

    fresh, fresh_bias = None, None
    if fresh_round is not None:
        fresh, shifts = refs["fresh"], rounds[fresh_round]
        units, known = fresh.shape[0], len(shifts)
        for unit in range(units):
            fresh[unit] = refs["rows"][unit] if unit < known else jnp.zeros(fresh.shape[1:], jnp.bfloat16)
        place_of = lax.broadcasted_iota(jnp.int32, (padded, units * page), 1)
        asker = lax.broadcasted_iota(jnp.int32, (padded, units * page), 0)
        inside = remainder(place_of, page)
        token = jnp.full_like(place_of, 2 * padded)
        for unit, shift in enumerate(shifts):
            here = (place_of >= unit * page) & (place_of < (unit + 1) * page) & (inside < local_new)
            token = jnp.where(here, (rank ^ shift) * local_new + inside, token)
        if first:
            mine = lax.div(rank, ways // KVH)
            fresh[known, :, 0:HD] = refs["decode"][:, pl.ds(pl.multiple_of(mine * HD, HD), HD)]
            fresh[known, :, HD:] = refs["decode"][:, pl.ds(pl.multiple_of((KVH + mine) * HD, HD), HD)]
            here = (place_of >= known * page) & (place_of < (known + 1) * page) & (inside < decode)
            token = jnp.where(here, ways * local_new + inside, token)
        fresh_bias = jnp.where(token <= asker, 0.0, FLOOR).astype(jnp.float32)

    slope = HD ** -0.5 * math.log2(math.e)
    block_heads = min(heads, 4)
    tall = block_heads * padded

    def fold(state, query, key, value, bias):
        total, top, mixed = state
        score = lax.dot_general(query, key, (((1,), (1,)), ((), ())), preferred_element_type=jnp.float32) + bias
        new_top = jnp.maximum(top, jnp.max(score, axis=1, keepdims=True))
        weight = jnp.exp2((score - new_top) * slope)
        upper = weight.astype(jnp.bfloat16)
        lower = (weight - upper.astype(jnp.float32)).astype(jnp.bfloat16)
        wide = jnp.concatenate([value, jnp.ones_like(value)], axis=1)
        product = jnp.dot(upper, wide, preferred_element_type=jnp.float32)
        product = product + jnp.dot(lower, wide, preferred_element_type=jnp.float32)
        shrink = jnp.exp2((top - new_top) * slope)
        return total * shrink + product[:, HD:], new_top, mixed * shrink + product[:, :HD]

    blocks = dict(zip(stages[number], refs["blocks"]))
    for b in range(heads // block_heads):
        at = pl.ds(b * tall, tall)
        query = stacked[at, :]
        if first:
            state = (jnp.zeros((tall, HD), jnp.float32), jnp.full((tall, 1), FLOOR, jnp.float32),
                     jnp.zeros((tall, HD), jnp.float32))
        else:
            both = refs["carry"][0][at, :]
            state = (both[:, HD // 2:HD // 2 + 1], both[:, :1], refs["carry"][1][at, :])
        for n, (chunk, mask) in enumerate(zip(chunks, masks)):
            def rows_of(low):
                rows_here = [blocks[r, far][i, 0:capacity, :, low:low + HD].reshape(capacity * page, HD) for r, far, i in chunk]
                if fresh is not None and n == 0:
                    rows_here.append(fresh[:, :, low:low + HD].reshape(units * page, HD))
                return jnp.concatenate(rows_here, axis=0)

            bias = mask
            if fresh is not None and n == 0:
                bias = jnp.concatenate([jnp.broadcast_to(mask, (padded, mask.shape[1])), fresh_bias], axis=1)
                bias = jnp.concatenate([bias] * block_heads, axis=0)
            state = fold(state, query, rows_of(0), rows_of(HD), bias)
        if last:
            result = (state[2] / state[0]).astype(jnp.bfloat16)
            for h in range(block_heads):
                head = b * block_heads + h
                refs["out"][:, head * HD:(head + 1) * HD] = result[h * padded:h * padded + rows, :]
        else:
            left = lax.broadcasted_iota(jnp.int32, (tall, HD), 1) < HD // 2
            refs["next"][0][at, :] = jnp.where(left, state[1], state[0])
            refs["next"][1][at, :] = state[2]

    for chosen, home in homeward:
        @pl.when(chosen)
        def finish():
            for copy in home:
                copy.wait()


def on_device(queries, new_kv, decode_kv, pool, hist_pages, owner, block_table):
    groups, ways = lax.axis_size("grp"), lax.axis_size("tp")
    slots, page, features = pool.shape
    capacity = slots // groups
    span = groups * ways
    rows = queries.shape[1]
    heads = H // ways
    local_new = new_kv.shape[1]
    decode = decode_kv.shape[1]
    width = features // ways
    pages_in_all = groups * block_table.shape[1] // 2
    packed = min(slots, (pages_in_all + groups * (span - 1) - ways * groups * (groups - 1) // 2) // span)
    rounds = [list(reversed(range(3 * ways // 4))), list(reversed(range(3 * ways // 4, ways)))]
    stages = [[(0, far) for far in range(groups // 2)], [(0, far) for far in range(groups // 2, groups)], [(1, far) for far in range(groups // 2, groups)] + [(1, far) for far in range(groups // 2)]]
    params = pltpu.CompilerParams(vmem_limit_bytes=LIMIT)
    cheap = pl.CostEstimate(flops=0, bytes_accessed=0, transcendentals=0)

    new_rows = new_kv[0]
    if local_new < page:
        new_rows = jnp.pad(new_rows, ((0, page - local_new), (0, 0)))
    decode_rows = jnp.pad(decode_kv[0], ((0, page - decode), (0, 0)))

    unit = (page, 2 * HD)
    cut = pl.pallas_call(
        functools.partial(pack_kernel, (groups, ways, capacity, packed, page, width)),
        out_shape=[jax.ShapeDtypeStruct((packed + 2,) + unit, jnp.bfloat16)] * ways,
        in_specs=[SMEM, SMEM, SMEM, ANY, VMEM],
        out_specs=[VMEM] * ways,
        scratch_shapes=[pltpu.VMEM((packed, page, features), jnp.bfloat16), pltpu.SemaphoreType.DMA((packed,))],
        compiler_params=params,
        cost_estimate=cheap,
    )(hist_pages, owner, block_table, pool, new_rows)
    def along_tp(shift):
        return lax.ppermute(cut[shift], "tp", [(i, i ^ shift) for i in range(ways)])

    arrived = {0: cut[0]}
    arrived.update({shift: along_tp(shift) for shift in sorted(rounds[0]) if shift})

    def sort(shifts, before):
        sent = pl.pallas_call(
            functools.partial(regroup_kernel, (groups, ways, capacity, packed), shifts),
            out_shape=[jax.ShapeDtypeStruct((len(shifts), capacity + 1) + unit, jnp.bfloat16)] * groups + [
                jax.ShapeDtypeStruct((len(shifts),) + unit, jnp.bfloat16)],
            in_specs=[SMEM, SMEM] + [VMEM] * len(shifts) + [ANY] * len(before),
            out_specs=[VMEM] * (groups + 1),
            compiler_params=params,
            cost_estimate=cheap,
        )(hist_pages, owner, *[arrived[shift] for shift in shifts], *before)
        got = {far: lax.ppermute(sent[far], "grp", [(i, i ^ far) for i in range(groups)])
               for far in reversed(range(1, groups))}
        return [sent[0]] + [got[far] for far in range(1, groups)], sent[groups]

    tall = heads * (-(-rows // 16) * 16)
    def attend(number, carry):
        stage = stages[number]
        first, last = number == 0, number == len(stages) - 1
        args = dict(hist=hist_pages, owner=owner, query=queries[0], blocks=[parts[r][far] for r, far in stage])
        specs = dict(hist=SMEM, owner=SMEM, query=VMEM, blocks=[VMEM] * len(stage))
        scratch = dict(stacked=pltpu.VMEM((tall, HD), jnp.bfloat16))
        if first:
            args["decode"], specs["decode"] = decode_rows, VMEM
        if carry is not None:
            args["carry"], specs["carry"] = list(carry), [VMEM] * 2
        if first or last:
            args["rows"], specs["rows"] = fresh_rows[0 if first else 1], VMEM
            scratch["fresh"] = pltpu.VMEM((-(-(len(rounds[0 if first else 1]) + 1) // 8) * 8,) + unit, jnp.bfloat16)
        if last:
            args["parts"], specs["parts"] = parts, [[ANY] * groups for unused in rounds]
            outs = dict(out=jax.ShapeDtypeStruct((rows, heads * HD), jnp.bfloat16),
                        returned=jax.ShapeDtypeStruct((ways,) + unit, jnp.bfloat16))
            out_specs = dict(out=VMEM, returned=VMEM)
            scratch["home"] = pltpu.SemaphoreType.DMA((ways,))
        else:
            outs = dict(next=[jax.ShapeDtypeStruct((tall, HD), jnp.float32)] * 2)
            out_specs = dict(next=[VMEM] * 2)
        flat_args, in_tree = jax.tree.flatten(args)
        flat_outs, out_tree = jax.tree.flatten(outs)
        flat_scratch, scratch_tree = jax.tree.flatten(scratch)

        def kernel(*flat, in_tree=in_tree, out_tree=out_tree, scratch_tree=scratch_tree, number=number):
            n, m = in_tree.num_leaves, out_tree.num_leaves
            refs = dict(jax.tree.unflatten(in_tree, flat[:n]))
            refs.update(jax.tree.unflatten(out_tree, flat[n:n + m]))
            refs.update(jax.tree.unflatten(scratch_tree, flat[n + m:]))
            dims = (groups, ways, capacity, packed, page, rows, heads, local_new, decode)
            attend_kernel(dims, refs, rounds, stages, number)

        flat = pl.pallas_call(
            kernel,
            out_shape=flat_outs,
            in_specs=jax.tree.leaves(specs),
            out_specs=jax.tree.leaves(out_specs),
            scratch_shapes=flat_scratch,
            compiler_params=params,
            cost_estimate=cheap,
        )(*flat_args)
        result = jax.tree.unflatten(out_tree, flat)
        return result

    (near_parts, near_fresh) = sort(rounds[0], [])
    arrived.update({shift: along_tp(shift) for shift in rounds[1]})
    parts, fresh_rows = [near_parts], [near_fresh]
    result = attend(0, None)
    (far_parts, far_fresh) = sort(rounds[1], [result["next"][0]])
    parts.append(far_parts)
    fresh_rows.append(far_fresh)
    for number in range(1, len(stages)):
        result = attend(number, result["next"])
    returned = result["returned"][:, :local_new, :width].reshape(1, ways * local_new, width)
    return result["out"][None], returned


def solution(mesh):
    return jax.shard_map(
        on_device,
        mesh=mesh,
        in_specs=(
            P("grp", None, "tp"),
            P("grp", "tp", None),
            P("grp", None, None),
            P(("grp", "tp"), None, None),
            P(),
            P(),
            P(),
        ),
        out_specs=(P("grp", None, "tp"), P("grp", None, "tp")),
        check_vma=False,
    )
```

```python
import functools
import math

import jax
import jax.numpy as jnp
from jax import lax
from jax.experimental import pallas as pl
from jax.experimental.pallas import tpu as pltpu
from jax.sharding import PartitionSpec as P

H = 64
KVH = 8
HD = 128
FLOOR = -1e30
ANY = pl.BlockSpec(memory_space=pl.ANY)
SMEM = pl.BlockSpec(memory_space=pltpu.SMEM)
VMEM = pl.BlockSpec(memory_space=pltpu.VMEM)
LIMIT = 32 * 1024 * 1024


def divide(value, by):
    if by & (by - 1):
        return lax.div(value, by)
    return lax.shift_right_logical(value, by.bit_length() - 1)


def remainder(value, by):
    if by & (by - 1):
        return lax.rem(value, by)
    return value & (by - 1)


def live_pages(session, group, rank, hist_ref, owner_ref, groups, ways):
    step = groups * ways
    first = remainder(group - owner_ref[session] + groups, groups) * ways + rank
    return divide(hist_ref[session] - first + step - 1, step)


def place(session, group, rank, hist_ref, owner_ref, groups, ways):
    def add(s, total):
        n = live_pages(s, group, rank, hist_ref, owner_ref, groups, ways)
        return total + jnp.where(s < session, n, 0)

    offset = lax.fori_loop(0, groups, add, jnp.int32(0), unroll=groups <= 4)
    return offset, live_pages(session, group, rank, hist_ref, owner_ref, groups, ways)


def pack_kernel(dims, hist_ref, owner_ref, table_ref, pool_ref, new_ref, *refs):
    groups, ways, capacity, packed, page, width = dims
    outs, stage, sem = refs[:ways], refs[ways], refs[ways + 1]
    group, rank = lax.axis_index("grp"), lax.axis_index("tp")
    def each_session(s, at):
        first = remainder(group - owner_ref[s] + groups, groups) * ways + rank
        count = live_pages(s, group, rank, hist_ref, owner_ref, groups, ways)

        def each_page(j, at):
            slot = table_ref[s, j * groups * ways + first]
            pltpu.make_async_copy(pool_ref.at[slot], stage.at[at], sem.at[at]).start()
            return at + 1

        return lax.fori_loop(0, count, each_page, at)

    total = lax.fori_loop(0, groups, each_session, jnp.int32(0))
    repeat = ways // KVH

    def halves(shift):
        to = rank ^ shift
        key = pl.multiple_of(lax.div(to, repeat) * HD, HD)
        value = pl.multiple_of((KVH + lax.div(to, repeat)) * HD, HD)
        return to, key, value

    for shift in range(ways):
        to, key, value = halves(shift)
        outs[shift][packed, :, 0:HD] = new_ref[:, pl.ds(key, HD)]
        outs[shift][packed, :, HD:] = new_ref[:, pl.ds(value, HD)]
        columns = pl.multiple_of(to * width, width)
        outs[shift][packed + 1, :, 0:width] = new_ref[:, pl.ds(columns, width)]

    def blank(i, unused):
        stage[i] = jnp.zeros(stage.shape[1:], stage.dtype)
        return unused

    lax.fori_loop(total, packed, blank, 0)

    def drain(i, unused):
        pltpu.make_async_copy(pool_ref.at[0], stage.at[i], sem.at[i]).wait()
        return unused

    lax.fori_loop(0, total, drain, 0)

    for shift in range(ways):
        to, key, value = halves(shift)
        outs[shift][0:packed, :, 0:HD] = stage[:, :, pl.ds(key, HD)]
        outs[shift][0:packed, :, HD:] = stage[:, :, pl.ds(value, HD)]


def regroup_kernel(dims, shifts, hist_ref, owner_ref, *refs):
    groups, ways, capacity, packed = dims
    count = len(shifts)
    ins, outs, fresh = refs[:count], refs[-groups - 1:-1], refs[-1]
    group, rank = lax.axis_index("grp"), lax.axis_index("tp")
    for i, shift in enumerate(shifts):
        for far in range(groups):
            offset, unused = place(group ^ far, group, rank ^ shift, hist_ref, owner_ref, groups, ways)
            start = jnp.minimum(offset, packed + 2 - capacity)
            outs[far][i, 0:capacity] = ins[i][pl.ds(start, capacity)]
            outs[far][i, capacity] = ins[i][packed + 1]
        fresh[i] = ins[i][packed]


def attend_kernel(dims, refs, rounds, stages, number):
    groups, ways, capacity, packed, page, rows, heads, local_new, decode = dims
    first, last = number == 0, number == len(stages) - 1
    fresh_round = 0 if first else 1 if last else None
    hist_ref, owner_ref, query_ref = refs["hist"], refs["owner"], refs["query"]
    padded = -(-rows // 16) * 16
    group, rank = lax.axis_index("grp"), lax.axis_index("tp")
    stacked = refs["stacked"]

    homeward = []
    if last:
        sender = jnp.int32(0)
        for s in range(groups):
            sender = sender + jnp.where(owner_ref[s] == group, s, 0)
        for far in range(groups):
            home = [pltpu.make_async_copy(
                refs["parts"][r][far].at[i, capacity], refs["returned"].at[rank ^ shift], refs["home"].at[shift])
                for r, sources in enumerate(rounds) for i, shift in enumerate(sources)]
            homeward.append(((sender ^ group) == far, home))

            @pl.when(homeward[far][0])
            def start():
                for copy in homeward[far][1]:
                    copy.start()

    for head in range(heads):
        stacked[head * padded:head * padded + rows, :] = query_ref[:, head * HD:(head + 1) * HD]
        stacked[head * padded + rows:(head + 1) * padded, :] = jnp.zeros((padded - rows, HD), jnp.bfloat16)

    items = [(r, far, i) for r, far in stages[number] for i in range(len(rounds[r]))]
    many = -(-len(items) // -(-len(items) // 12))
    many = -(-many // 4) * 4
    chunks = [items[k:k + many] for k in range(0, len(items), many)]
    masks = []
    for chunk in chunks:
        lane = lax.broadcasted_iota(jnp.int32, (1, len(chunk) * capacity * page), 1)
        seen = lane < 0
        for n, (r, far, i) in enumerate(chunk):
            offset, live = place(group, group ^ far, rank ^ rounds[r][i], hist_ref, owner_ref, groups, ways)
            low = (n * capacity + offset - jnp.minimum(offset, packed + 2 - capacity)) * page
            seen = seen | ((lane >= low) & (lane < low + live * page))
        masks.append(jnp.where(seen, 0.0, FLOOR).astype(jnp.float32))

    fresh, fresh_bias = None, None
    if fresh_round is not None:
        fresh, shifts = refs["fresh"], rounds[fresh_round]
        units, known = fresh.shape[0], len(shifts)
        for unit in range(units):
            fresh[unit] = refs["rows"][unit] if unit < known else jnp.zeros(fresh.shape[1:], jnp.bfloat16)
        place_of = lax.broadcasted_iota(jnp.int32, (padded, units * page), 1)
        asker = lax.broadcasted_iota(jnp.int32, (padded, units * page), 0)
        inside = remainder(place_of, page)
        token = jnp.full_like(place_of, 2 * padded)
        for unit, shift in enumerate(shifts):
            here = (place_of >= unit * page) & (place_of < (unit + 1) * page) & (inside < local_new)
            token = jnp.where(here, (rank ^ shift) * local_new + inside, token)
        if first:
            mine = lax.div(rank, ways // KVH)
            fresh[known, :, 0:HD] = refs["decode"][:, pl.ds(pl.multiple_of(mine * HD, HD), HD)]
            fresh[known, :, HD:] = refs["decode"][:, pl.ds(pl.multiple_of((KVH + mine) * HD, HD), HD)]
            here = (place_of >= known * page) & (place_of < (known + 1) * page) & (inside < decode)
            token = jnp.where(here, ways * local_new + inside, token)
        fresh_bias = jnp.where(token <= asker, 0.0, FLOOR).astype(jnp.float32)

    slope = HD ** -0.5 * math.log2(math.e)
    block_heads = min(heads, 4)
    tall = block_heads * padded

    def fold(state, query, key, value, bias):
        total, top, mixed = state
        score = lax.dot_general(query, key, (((1,), (1,)), ((), ())), preferred_element_type=jnp.float32) + bias
        new_top = jnp.maximum(top, jnp.max(score, axis=1, keepdims=True))
        weight = jnp.exp2((score - new_top) * slope)
        upper = weight.astype(jnp.bfloat16)
        lower = (weight - upper.astype(jnp.float32)).astype(jnp.bfloat16)
        wide = jnp.concatenate([value, jnp.ones_like(value)], axis=1)
        product = jnp.dot(upper, wide, preferred_element_type=jnp.float32)
        product = product + jnp.dot(lower, wide, preferred_element_type=jnp.float32)
        shrink = jnp.exp2((top - new_top) * slope)
        return total * shrink + product[:, HD:], new_top, mixed * shrink + product[:, :HD]

    blocks = dict(zip(stages[number], refs["blocks"]))
    for b in range(heads // block_heads):
        at = pl.ds(b * tall, tall)
        query = stacked[at, :]
        if first:
            state = (jnp.zeros((tall, HD), jnp.float32), jnp.full((tall, 1), FLOOR, jnp.float32),
                     jnp.zeros((tall, HD), jnp.float32))
        else:
            both = refs["carry"][0][at, :]
            state = (both[:, HD // 2:HD // 2 + 1], both[:, :1], refs["carry"][1][at, :])
        for n, (chunk, mask) in enumerate(zip(chunks, masks)):
            def rows_of(low):
                rows_here = [blocks[r, far][i, 0:capacity, :, low:low + HD].reshape(capacity * page, HD) for r, far, i in chunk]
                if fresh is not None and n == 0:
                    rows_here.append(fresh[:, :, low:low + HD].reshape(units * page, HD))
                return jnp.concatenate(rows_here, axis=0)

            bias = mask
            if fresh is not None and n == 0:
                bias = jnp.concatenate([jnp.broadcast_to(mask, (padded, mask.shape[1])), fresh_bias], axis=1)
                bias = jnp.concatenate([bias] * block_heads, axis=0)
            state = fold(state, query, rows_of(0), rows_of(HD), bias)
        if last:
            result = (state[2] / state[0]).astype(jnp.bfloat16)
            for h in range(block_heads):
                head = b * block_heads + h
                refs["out"][:, head * HD:(head + 1) * HD] = result[h * padded:h * padded + rows, :]
        else:
            left = lax.broadcasted_iota(jnp.int32, (tall, HD), 1) < HD // 2
            refs["next"][0][at, :] = jnp.where(left, state[1], state[0])
            refs["next"][1][at, :] = state[2]

    for chosen, home in homeward:
        @pl.when(chosen)
        def finish():
            for copy in home:
                copy.wait()


def on_device(queries, new_kv, decode_kv, pool, hist_pages, owner, block_table):
    groups, ways = lax.axis_size("grp"), lax.axis_size("tp")
    slots, page, features = pool.shape
    capacity = slots // groups
    span = groups * ways
    rows = queries.shape[1]
    heads = H // ways
    local_new = new_kv.shape[1]
    decode = decode_kv.shape[1]
    width = features // ways
    pages_in_all = groups * block_table.shape[1] // 2
    packed = min(slots, (pages_in_all + groups * (span - 1) - ways * groups * (groups - 1) // 2) // span)
    rounds = [list(reversed(range(3 * ways // 4))), list(reversed(range(3 * ways // 4, ways)))]
    stages = [[(0, far) for far in range(groups // 2)], [(0, far) for far in range(groups // 2, groups)] + [(1, far) for far in range(groups // 2)], [(1, far) for far in range(groups // 2, groups)]]
    params = pltpu.CompilerParams(vmem_limit_bytes=LIMIT)
    cheap = pl.CostEstimate(flops=0, bytes_accessed=0, transcendentals=0)

    new_rows = new_kv[0]
    if local_new < page:
        new_rows = jnp.pad(new_rows, ((0, page - local_new), (0, 0)))
    decode_rows = jnp.pad(decode_kv[0], ((0, page - decode), (0, 0)))

    unit = (page, 2 * HD)
    cut = pl.pallas_call(
        functools.partial(pack_kernel, (groups, ways, capacity, packed, page, width)),
        out_shape=[jax.ShapeDtypeStruct((packed + 2,) + unit, jnp.bfloat16)] * ways,
        in_specs=[SMEM, SMEM, SMEM, ANY, VMEM],
        out_specs=[VMEM] * ways,
        scratch_shapes=[pltpu.VMEM((packed, page, features), jnp.bfloat16), pltpu.SemaphoreType.DMA((packed,))],
        compiler_params=pltpu.CompilerParams(vmem_limit_bytes=56 * 1024 * 1024),
        cost_estimate=cheap,
    )(hist_pages, owner, block_table, pool, new_rows)
    def along_tp(shift):
        return lax.ppermute(cut[shift], "tp", [(i, i ^ shift) for i in range(ways)])

    arrived = {0: cut[0]}
    arrived.update({shift: along_tp(shift) for shift in sorted(rounds[0]) if shift})

    def sort(shifts, before):
        sent = pl.pallas_call(
            functools.partial(regroup_kernel, (groups, ways, capacity, packed), shifts),
            out_shape=[jax.ShapeDtypeStruct((len(shifts), capacity + 1) + unit, jnp.bfloat16)] * groups + [
                jax.ShapeDtypeStruct((len(shifts),) + unit, jnp.bfloat16)],
            in_specs=[SMEM, SMEM] + [VMEM] * len(shifts) + [ANY] * len(before),
            out_specs=[VMEM] * (groups + 1),
            compiler_params=params,
            cost_estimate=cheap,
        )(hist_pages, owner, *[arrived[shift] for shift in shifts], *before)
        got = {far: lax.ppermute(sent[far], "grp", [(i, i ^ far) for i in range(groups)])
               for far in reversed(range(1, groups))}
        return [sent[0]] + [got[far] for far in range(1, groups)], sent[groups]

    tall = heads * (-(-rows // 16) * 16)
    def attend(number, carry):
        stage = stages[number]
        first, last = number == 0, number == len(stages) - 1
        args = dict(hist=hist_pages, owner=owner, query=queries[0], blocks=[parts[r][far] for r, far in stage])
        specs = dict(hist=SMEM, owner=SMEM, query=VMEM, blocks=[VMEM] * len(stage))
        scratch = dict(stacked=pltpu.VMEM((tall, HD), jnp.bfloat16))
        if first:
            args["decode"], specs["decode"] = decode_rows, VMEM
        if carry is not None:
            args["carry"], specs["carry"] = list(carry), [VMEM] * 2
        if first or last:
            args["rows"], specs["rows"] = fresh_rows[0 if first else 1], VMEM
            scratch["fresh"] = pltpu.VMEM((-(-(len(rounds[0 if first else 1]) + 1) // 8) * 8,) + unit, jnp.bfloat16)
        if last:
            args["parts"], specs["parts"] = parts, [[ANY] * groups for unused in rounds]
            outs = dict(out=jax.ShapeDtypeStruct((rows, heads * HD), jnp.bfloat16),
                        returned=jax.ShapeDtypeStruct((ways,) + unit, jnp.bfloat16))
            out_specs = dict(out=VMEM, returned=VMEM)
            scratch["home"] = pltpu.SemaphoreType.DMA((ways,))
        else:
            outs = dict(next=[jax.ShapeDtypeStruct((tall, HD), jnp.float32)] * 2)
            out_specs = dict(next=[VMEM] * 2)
        flat_args, in_tree = jax.tree.flatten(args)
        flat_outs, out_tree = jax.tree.flatten(outs)
        flat_scratch, scratch_tree = jax.tree.flatten(scratch)

        def kernel(*flat, in_tree=in_tree, out_tree=out_tree, scratch_tree=scratch_tree, number=number):
            n, m = in_tree.num_leaves, out_tree.num_leaves
            refs = dict(jax.tree.unflatten(in_tree, flat[:n]))
            refs.update(jax.tree.unflatten(out_tree, flat[n:n + m]))
            refs.update(jax.tree.unflatten(scratch_tree, flat[n + m:]))
            dims = (groups, ways, capacity, packed, page, rows, heads, local_new, decode)
            attend_kernel(dims, refs, rounds, stages, number)

        flat = pl.pallas_call(
            kernel,
            out_shape=flat_outs,
            in_specs=jax.tree.leaves(specs),
            out_specs=jax.tree.leaves(out_specs),
            scratch_shapes=flat_scratch,
            compiler_params=params,
            cost_estimate=cheap,
        )(*flat_args)
        result = jax.tree.unflatten(out_tree, flat)
        return result

    (near_parts, near_fresh) = sort(rounds[0], [])
    arrived.update({shift: along_tp(shift) for shift in rounds[1]})
    parts, fresh_rows = [near_parts], [near_fresh]
    result = attend(0, None)
    (far_parts, far_fresh) = sort(rounds[1], [result["next"][0]])
    parts.append(far_parts)
    fresh_rows.append(far_fresh)
    for number in range(1, len(stages)):
        result = attend(number, result["next"])
    returned = result["returned"][:, :local_new, :width].reshape(1, ways * local_new, width)
    return result["out"][None], returned


def solution(mesh):
    return jax.shard_map(
        on_device,
        mesh=mesh,
        in_specs=(
            P("grp", None, "tp"),
            P("grp", "tp", None),
            P("grp", None, None),
            P(("grp", "tp"), None, None),
            P(),
            P(),
            P(),
        ),
        out_specs=(P("grp", None, "tp"), P("grp", None, "tp")),
        check_vma=False,
    )
```

```python
import functools
import math

import jax
import jax.numpy as jnp
from jax import lax
from jax.experimental import pallas as pl
from jax.experimental.pallas import tpu as pltpu
from jax.sharding import PartitionSpec as P

H = 64
KVH = 8
HD = 128
FLOOR = -1e30
ANY = pl.BlockSpec(memory_space=pl.ANY)
SMEM = pl.BlockSpec(memory_space=pltpu.SMEM)
VMEM = pl.BlockSpec(memory_space=pltpu.VMEM)
LIMIT = 32 * 1024 * 1024


def divide(value, by):
    if by & (by - 1):
        return lax.div(value, by)
    return lax.shift_right_logical(value, by.bit_length() - 1)


def remainder(value, by):
    if by & (by - 1):
        return lax.rem(value, by)
    return value & (by - 1)


def live_pages(session, group, rank, hist_ref, owner_ref, groups, ways):
    step = groups * ways
    first = remainder(group - owner_ref[session] + groups, groups) * ways + rank
    return divide(hist_ref[session] - first + step - 1, step)


def place(session, group, rank, hist_ref, owner_ref, groups, ways):
    def add(s, total):
        n = live_pages(s, group, rank, hist_ref, owner_ref, groups, ways)
        return total + jnp.where(s < session, n, 0)

    offset = lax.fori_loop(0, groups, add, jnp.int32(0), unroll=groups <= 4)
    return offset, live_pages(session, group, rank, hist_ref, owner_ref, groups, ways)


def pack_kernel(dims, hist_ref, owner_ref, table_ref, pool_ref, new_ref, *refs):
    groups, ways, capacity, packed, page, width = dims
    outs, stage, sem = refs[:ways], refs[ways], refs[ways + 1]
    group, rank = lax.axis_index("grp"), lax.axis_index("tp")
    def each_session(s, at):
        first = remainder(group - owner_ref[s] + groups, groups) * ways + rank
        count = live_pages(s, group, rank, hist_ref, owner_ref, groups, ways)

        def each_page(j, at):
            slot = table_ref[s, j * groups * ways + first]
            pltpu.make_async_copy(pool_ref.at[slot], stage.at[at], sem.at[at]).start()
            return at + 1

        return lax.fori_loop(0, count, each_page, at)

    total = lax.fori_loop(0, groups, each_session, jnp.int32(0))
    repeat = ways // KVH

    def halves(shift):
        to = rank ^ shift
        key = pl.multiple_of(lax.div(to, repeat) * HD, HD)
        value = pl.multiple_of((KVH + lax.div(to, repeat)) * HD, HD)
        return to, key, value

    for shift in range(ways):
        to, key, value = halves(shift)
        outs[shift][packed, :, 0:HD] = new_ref[:, pl.ds(key, HD)]
        outs[shift][packed, :, HD:] = new_ref[:, pl.ds(value, HD)]
        columns = pl.multiple_of(to * width, width)
        outs[shift][packed + 1, :, 0:width] = new_ref[:, pl.ds(columns, width)]

    def blank(i, unused):
        stage[i] = jnp.zeros(stage.shape[1:], stage.dtype)
        return unused

    lax.fori_loop(total, packed, blank, 0)

    def drain(i, unused):
        pltpu.make_async_copy(pool_ref.at[0], stage.at[i], sem.at[i]).wait()
        return unused

    lax.fori_loop(0, total, drain, 0)

    for shift in range(ways):
        to, key, value = halves(shift)
        outs[shift][0:packed, :, 0:HD] = stage[:, :, pl.ds(key, HD)]
        outs[shift][0:packed, :, HD:] = stage[:, :, pl.ds(value, HD)]


def regroup_kernel(dims, shifts, hist_ref, owner_ref, *refs):
    groups, ways, capacity, packed = dims
    count = len(shifts)
    ins, outs, fresh = refs[:count], refs[-groups - 1:-1], refs[-1]
    group, rank = lax.axis_index("grp"), lax.axis_index("tp")
    for i, shift in enumerate(shifts):
        for far in range(groups):
            offset, unused = place(group ^ far, group, rank ^ shift, hist_ref, owner_ref, groups, ways)
            start = jnp.minimum(offset, packed + 2 - capacity)
            outs[far][i, 0:capacity] = ins[i][pl.ds(start, capacity)]
            outs[far][i, capacity] = ins[i][packed + 1]
        fresh[i] = ins[i][packed]


def attend_kernel(dims, refs, rounds, stages, number):
    groups, ways, capacity, packed, page, rows, heads, local_new, decode = dims
    first, last = number == 0, number == len(stages) - 1
    fresh_rounds = rounds[:-1] if first else rounds[-1:] if number == 1 else []
    hist_ref, owner_ref, query_ref = refs["hist"], refs["owner"], refs["query"]
    padded = -(-rows // 8) * 8
    group, rank = lax.axis_index("grp"), lax.axis_index("tp")
    stacked = refs["stacked"]

    homeward = []
    if last:
        sender = jnp.int32(0)
        for s in range(groups):
            sender = sender + jnp.where(owner_ref[s] == group, s, 0)
        for far in range(groups):
            home = [pltpu.make_async_copy(
                refs["parts"][r][far].at[i, capacity], refs["returned"].at[rank ^ shift], refs["home"].at[shift])
                for r, sources in enumerate(rounds) for i, shift in enumerate(sources)]
            homeward.append(((sender ^ group) == far, home))

            @pl.when(homeward[far][0])
            def start():
                for copy in homeward[far][1]:
                    copy.start()

    for head in range(heads):
        stacked[head * padded:head * padded + rows, :] = query_ref[:, head * HD:(head + 1) * HD].astype(jnp.float32)
        stacked[head * padded + rows:(head + 1) * padded, :] = jnp.zeros((padded - rows, HD), jnp.float32)

    items = [(r, far, i) for r, far in stages[number] for i in range(len(rounds[r]))]
    many = -(-len(items) // -(-len(items) // 12))
    many = -(-many // 4) * 4
    chunks = [items[k:k + many] for k in range(0, len(items), many)]
    masks = []
    for chunk in chunks:
        lane = lax.broadcasted_iota(jnp.int32, (1, len(chunk) * capacity * page), 1)
        seen = lane < 0
        for n, (r, far, i) in enumerate(chunk):
            offset, live = place(group, group ^ far, rank ^ rounds[r][i], hist_ref, owner_ref, groups, ways)
            low = (n * capacity + offset - jnp.minimum(offset, packed + 2 - capacity)) * page
            seen = seen | ((lane >= low) & (lane < low + live * page))
        masks.append(jnp.where(seen, 0.0, FLOOR).astype(jnp.float32))

    fresh, fresh_bias = None, None
    if fresh_rounds:
        fresh, shifts = refs["fresh"], [shift for shifts in fresh_rounds for shift in shifts]
        given = [ref.at[i] for shifts, ref in zip(fresh_rounds, refs["rows"]) for i in range(len(shifts))]
        units, known = fresh.shape[0], len(shifts)
        for unit in range(units):
            fresh[unit] = given[unit][...] if unit < known else jnp.zeros(fresh.shape[1:], jnp.bfloat16)
        place_of = lax.broadcasted_iota(jnp.int32, (padded, units * page), 1)
        asker = lax.broadcasted_iota(jnp.int32, (padded, units * page), 0)
        inside = remainder(place_of, page)
        token = jnp.full_like(place_of, 2 * padded)
        for unit, shift in enumerate(shifts):
            here = (place_of >= unit * page) & (place_of < (unit + 1) * page) & (inside < local_new)
            token = jnp.where(here, (rank ^ shift) * local_new + inside, token)
        if first:
            mine = lax.div(rank, ways // KVH)
            fresh[known, :, 0:HD] = refs["decode"][:, pl.ds(pl.multiple_of(mine * HD, HD), HD)]
            fresh[known, :, HD:] = refs["decode"][:, pl.ds(pl.multiple_of((KVH + mine) * HD, HD), HD)]
            here = (place_of >= known * page) & (place_of < (known + 1) * page) & (inside < decode)
            token = jnp.where(here, ways * local_new + inside, token)
        fresh_bias = jnp.where(token <= asker, 0.0, FLOOR).astype(jnp.float32)

    slope = HD ** -0.5 * math.log2(math.e)
    block_heads = min(heads, 4)
    tall = block_heads * padded

    def fold(state, query, key, value, bias):
        total, top, mixed = state
        score = lax.dot_general(query, key, (((1,), (1,)), ((), ())), preferred_element_type=jnp.float32) + bias
        new_top = jnp.maximum(top, jnp.max(score, axis=1, keepdims=True))
        weight = jnp.exp2((score - new_top) * slope)
        upper = weight.astype(jnp.bfloat16)
        lower = (weight - upper.astype(jnp.float32)).astype(jnp.bfloat16)
        wide = jnp.concatenate([value, jnp.ones_like(value)], axis=1)
        product = jnp.dot(upper, wide, preferred_element_type=jnp.float32)
        product = product + jnp.dot(lower, wide, preferred_element_type=jnp.float32)
        shrink = jnp.exp2((top - new_top) * slope)
        return total * shrink + product[:, HD:], new_top, mixed * shrink + product[:, :HD]

    blocks = dict(zip(stages[number], refs["blocks"]))
    for b in range(heads // block_heads):
        at = pl.ds(b * tall, tall)
        query = stacked[at, :].astype(jnp.bfloat16)
        if first:
            state = (jnp.zeros((tall, HD), jnp.float32), jnp.full((tall, 1), FLOOR, jnp.float32),
                     jnp.zeros((tall, HD), jnp.float32))
        else:
            both = refs["carry"][0][at, :]
            state = (both[:, HD // 2:HD // 2 + 1], both[:, :1], refs["carry"][1][at, :])
        for n, (chunk, mask) in enumerate(zip(chunks, masks)):
            def rows_of(low):
                rows_here = [blocks[r, far][i, 0:capacity, :, low:low + HD].reshape(capacity * page, HD) for r, far, i in chunk]
                if fresh is not None and n == 0:
                    rows_here.append(fresh[:, :, low:low + HD].reshape(units * page, HD))
                return jnp.concatenate(rows_here, axis=0)

            bias = mask
            if fresh is not None and n == 0:
                bias = jnp.concatenate([jnp.broadcast_to(mask, (padded, mask.shape[1])), fresh_bias], axis=1)
                bias = jnp.concatenate([bias] * block_heads, axis=0)
            state = fold(state, query, rows_of(0), rows_of(HD), bias)
        if last:
            result = state[2] / state[0]
            for h in range(block_heads):
                head = b * block_heads + h
                refs["out"][:, head * HD:(head + 1) * HD] = result[h * padded:h * padded + rows, :].astype(jnp.bfloat16)
        else:
            left = lax.broadcasted_iota(jnp.int32, (tall, HD), 1) < HD // 2
            refs["next"][0][at, :] = jnp.where(left, state[1], state[0])
            refs["next"][1][at, :] = state[2]

    for chosen, home in homeward:
        @pl.when(chosen)
        def finish():
            for copy in home:
                copy.wait()


def on_device(queries, new_kv, decode_kv, pool, hist_pages, owner, block_table):
    groups, ways = lax.axis_size("grp"), lax.axis_size("tp")
    slots, page, features = pool.shape
    capacity = slots // groups
    span = groups * ways
    rows = queries.shape[1]
    heads = H // ways
    local_new = new_kv.shape[1]
    decode = decode_kv.shape[1]
    width = features // ways
    pages_in_all = groups * block_table.shape[1] // 2
    packed = min(slots, (pages_in_all + groups * (span - 1) - ways * groups * (groups - 1) // 2) // span)
    rounds = [list(reversed(range(3 * ways // 4))), list(reversed(range(3 * ways // 4, ways)))]
    stages = [
        [(r, far) for r in (0,) for far in range(groups // 2)],
        [(r, far) for r in (0,) for far in range(groups // 2, groups)] + [(r, far) for r in (1,) for far in range(groups // 2)],
        [(r, far) for r in (1,) for far in range(groups // 2, groups)]]
    params = pltpu.CompilerParams(vmem_limit_bytes=LIMIT)
    cheap = pl.CostEstimate(flops=0, bytes_accessed=0, transcendentals=0)

    new_rows = new_kv[0]
    if local_new < page:
        new_rows = jnp.pad(new_rows, ((0, page - local_new), (0, 0)))
    decode_rows = jnp.pad(decode_kv[0], ((0, page - decode), (0, 0)))

    unit = (page, 2 * HD)
    cut = pl.pallas_call(
        functools.partial(pack_kernel, (groups, ways, capacity, packed, page, width)),
        out_shape=[jax.ShapeDtypeStruct((packed + 2,) + unit, jnp.bfloat16)] * ways,
        in_specs=[SMEM, SMEM, SMEM, ANY, VMEM],
        out_specs=[VMEM] * ways,
        scratch_shapes=[pltpu.VMEM((packed, page, features), jnp.bfloat16), pltpu.SemaphoreType.DMA((packed,))],
        compiler_params=pltpu.CompilerParams(vmem_limit_bytes=56 * 1024 * 1024),
        cost_estimate=cheap,
    )(hist_pages, owner, block_table, pool, new_rows)
    def along_tp(shift):
        return lax.ppermute(cut[shift], "tp", [(i, i ^ shift) for i in range(ways)])

    arrived = {0: cut[0]}

    def sort(shifts, before):
        sent = pl.pallas_call(
            functools.partial(regroup_kernel, (groups, ways, capacity, packed), shifts),
            out_shape=[jax.ShapeDtypeStruct((len(shifts), capacity + 1) + unit, jnp.bfloat16)] * groups + [
                jax.ShapeDtypeStruct((len(shifts),) + unit, jnp.bfloat16)],
            in_specs=[SMEM, SMEM] + [VMEM] * len(shifts) + [ANY] * len(before),
            out_specs=[VMEM] * (groups + 1),
            compiler_params=params,
            cost_estimate=cheap,
        )(hist_pages, owner, *[arrived[shift] for shift in shifts], *before)
        got = {far: lax.ppermute(sent[far], "grp", [(i, i ^ far) for i in range(groups)])
               for far in reversed(range(1, groups))}
        return [sent[0]] + [got[far] for far in range(1, groups)], sent[groups]

    tall = heads * (-(-rows // 8) * 8)
    def attend(number, carry):
        stage = stages[number]
        first, last = number == 0, number == len(stages) - 1
        args = dict(hist=hist_pages, owner=owner, query=queries[0], blocks=[parts[r][far] for r, far in stage])
        specs = dict(hist=SMEM, owner=SMEM, query=VMEM, blocks=[VMEM] * len(stage))
        scratch = dict(stacked=pltpu.VMEM((tall, HD), jnp.float32))
        if first:
            args["decode"], specs["decode"] = decode_rows, VMEM
        if carry is not None:
            args["carry"], specs["carry"] = list(carry), [VMEM] * 2
        if number < 2:
            args["rows"] = list(fresh_rows) if first else fresh_rows[-1:]
            specs["rows"] = [VMEM] * len(args["rows"])
            some = sum(array.shape[0] for array in args["rows"])
            scratch["fresh"] = pltpu.VMEM((-(-(some + 1) // 8) * 8,) + unit, jnp.bfloat16)
        if last:
            args["parts"], specs["parts"] = parts, [[ANY] * groups for unused in rounds]
            outs = dict(out=jax.ShapeDtypeStruct((rows, heads * HD), jnp.bfloat16),
                        returned=jax.ShapeDtypeStruct((ways,) + unit, jnp.bfloat16))
            out_specs = dict(out=VMEM, returned=VMEM)
            scratch["home"] = pltpu.SemaphoreType.DMA((ways,))
        else:
            outs = dict(next=[jax.ShapeDtypeStruct((tall, HD), jnp.float32)] * 2)
            out_specs = dict(next=[VMEM] * 2)
        flat_args, in_tree = jax.tree.flatten(args)
        flat_outs, out_tree = jax.tree.flatten(outs)
        flat_scratch, scratch_tree = jax.tree.flatten(scratch)

        def kernel(*flat, in_tree=in_tree, out_tree=out_tree, scratch_tree=scratch_tree, number=number):
            n, m = in_tree.num_leaves, out_tree.num_leaves
            refs = dict(jax.tree.unflatten(in_tree, flat[:n]))
            refs.update(jax.tree.unflatten(out_tree, flat[n:n + m]))
            refs.update(jax.tree.unflatten(scratch_tree, flat[n + m:]))
            dims = (groups, ways, capacity, packed, page, rows, heads, local_new, decode)
            attend_kernel(dims, refs, rounds, stages, number)

        flat = pl.pallas_call(
            kernel,
            out_shape=flat_outs,
            in_specs=jax.tree.leaves(specs),
            out_specs=jax.tree.leaves(out_specs),
            scratch_shapes=flat_scratch,
            compiler_params=params,
            cost_estimate=cheap,
        )(*flat_args)
        result = jax.tree.unflatten(out_tree, flat)
        return result

    parts, fresh_rows, result = [], [], None
    for shifts in rounds:
        arrived.update({shift: along_tp(shift) for shift in sorted(shifts) if shift})
        if shifts == rounds[-1]:
            result = attend(0, None)
        sorted_pages, sorted_rows = sort(shifts, [] if result is None else [result["next"][0]])
        parts.append(sorted_pages)
        fresh_rows.append(sorted_rows)
    for number in range(1, len(stages)):
        result = attend(number, result["next"])
    returned = result["returned"][:, :local_new, :width].reshape(1, ways * local_new, width)
    return result["out"][None], returned


def solution(mesh):
    return jax.shard_map(
        on_device,
        mesh=mesh,
        in_specs=(
            P("grp", None, "tp"),
            P("grp", "tp", None),
            P("grp", None, None),
            P(("grp", "tp"), None, None),
            P(),
            P(),
            P(),
        ),
        out_specs=(P("grp", None, "tp"), P("grp", None, "tp")),
        check_vma=False,
    )
```

```python
import functools
import math

import jax
import jax.numpy as jnp
from jax import lax
from jax.experimental import pallas as pl
from jax.experimental.pallas import tpu as pltpu
from jax.sharding import PartitionSpec as P

H = 64
KVH = 8
HD = 128
FLOOR = -1e30
ANY = pl.BlockSpec(memory_space=pl.ANY)
SMEM = pl.BlockSpec(memory_space=pltpu.SMEM)
VMEM = pl.BlockSpec(memory_space=pltpu.VMEM)
LIMIT = 32 * 1024 * 1024


def divide(value, by):
    if by & (by - 1):
        return lax.div(value, by)
    return lax.shift_right_logical(value, by.bit_length() - 1)


def remainder(value, by):
    if by & (by - 1):
        return lax.rem(value, by)
    return value & (by - 1)


def live_pages(session, group, rank, hist_ref, owner_ref, groups, ways):
    step = groups * ways
    first = remainder(group - owner_ref[session] + groups, groups) * ways + rank
    return divide(hist_ref[session] - first + step - 1, step)


def place(session, group, rank, hist_ref, owner_ref, groups, ways):
    def add(s, total):
        n = live_pages(s, group, rank, hist_ref, owner_ref, groups, ways)
        return total + jnp.where(s < session, n, 0)

    offset = lax.fori_loop(0, groups, add, jnp.int32(0), unroll=groups <= 4)
    return offset, live_pages(session, group, rank, hist_ref, owner_ref, groups, ways)


def pack_kernel(dims, hist_ref, owner_ref, table_ref, pool_ref, new_ref, *refs):
    groups, ways, capacity, packed, page, width = dims
    outs, stage, sem = refs[:ways], refs[ways], refs[ways + 1]
    group, rank = lax.axis_index("grp"), lax.axis_index("tp")
    def each_session(s, at):
        first = remainder(group - owner_ref[s] + groups, groups) * ways + rank
        count = live_pages(s, group, rank, hist_ref, owner_ref, groups, ways)

        def each_page(j, at):
            slot = table_ref[s, j * groups * ways + first]
            pltpu.make_async_copy(pool_ref.at[slot], stage.at[at], sem.at[at]).start()
            return at + 1

        return lax.fori_loop(0, count, each_page, at)

    total = lax.fori_loop(0, groups, each_session, jnp.int32(0))
    repeat = ways // KVH

    def halves(shift):
        to = rank ^ shift
        key = pl.multiple_of(lax.div(to, repeat) * HD, HD)
        value = pl.multiple_of((KVH + lax.div(to, repeat)) * HD, HD)
        return to, key, value

    for shift in range(ways):
        to, key, value = halves(shift)
        outs[shift][packed, :, 0:HD] = new_ref[:, pl.ds(key, HD)]
        outs[shift][packed, :, HD:] = new_ref[:, pl.ds(value, HD)]
        columns = pl.multiple_of(to * width, width)
        outs[shift][packed + 1, :, 0:width] = new_ref[:, pl.ds(columns, width)]

    def blank(i, unused):
        stage[i] = jnp.zeros(stage.shape[1:], stage.dtype)
        return unused

    lax.fori_loop(total, packed, blank, 0)

    def drain(i, unused):
        pltpu.make_async_copy(pool_ref.at[0], stage.at[i], sem.at[i]).wait()
        return unused

    lax.fori_loop(0, total, drain, 0)

    for shift in range(ways):
        to, key, value = halves(shift)
        outs[shift][0:packed, :, 0:HD] = stage[:, :, pl.ds(key, HD)]
        outs[shift][0:packed, :, HD:] = stage[:, :, pl.ds(value, HD)]


def hold_kernel(own_ref, other_ref, out_ref, same_ref):
    out_ref[...] = own_ref[...]


def regroup_kernel(dims, shifts, hist_ref, owner_ref, *refs):
    groups, ways, capacity, packed = dims
    count = len(shifts)
    ins, outs, fresh = refs[:count], refs[-groups - 1:-1], refs[-1]
    group, rank = lax.axis_index("grp"), lax.axis_index("tp")
    for i, shift in enumerate(shifts):
        for far in range(groups):
            offset, unused = place(group ^ far, group, rank ^ shift, hist_ref, owner_ref, groups, ways)
            start = jnp.minimum(offset, packed + 2 - capacity)
            outs[far][i, 0:capacity] = ins[i][pl.ds(start, capacity)]
            outs[far][i, capacity] = ins[i][packed + 1]
        fresh[i] = ins[i][packed]


def attend_kernel(dims, refs, rounds, stages, number):
    groups, ways, capacity, packed, page, rows, heads, local_new, decode = dims
    first, last = number == 0, number == len(stages) - 1
    fresh_rounds = rounds[:-1] if first else rounds[-1:] if number == 1 else []
    hist_ref, owner_ref, query_ref = refs["hist"], refs["owner"], refs["query"]
    padded = -(-rows // 8) * 8
    group, rank = lax.axis_index("grp"), lax.axis_index("tp")
    stacked = refs["stacked"]

    homeward = []
    if last:
        sender = jnp.int32(0)
        for s in range(groups):
            sender = sender + jnp.where(owner_ref[s] == group, s, 0)
        for far in range(groups):
            home = [pltpu.make_async_copy(
                refs["parts"][r][far].at[i, capacity], refs["returned"].at[rank ^ shift], refs["home"].at[shift])
                for r, sources in enumerate(rounds) for i, shift in enumerate(sources)]
            homeward.append(((sender ^ group) == far, home))

            @pl.when(homeward[far][0])
            def start():
                for copy in homeward[far][1]:
                    copy.start()

    for head in range(heads):
        stacked[head * padded:head * padded + rows, :] = query_ref[:, head * HD:(head + 1) * HD].astype(jnp.float32)
        stacked[head * padded + rows:(head + 1) * padded, :] = jnp.zeros((padded - rows, HD), jnp.float32)

    items = [(r, far, i) for r, far in stages[number] for i in range(len(rounds[r]))]
    many = -(-len(items) // -(-len(items) // 12))
    many = -(-many // 4) * 4
    chunks = [items[k:k + many] for k in range(0, len(items), many)]
    masks = []
    for chunk in chunks:
        lane = lax.broadcasted_iota(jnp.int32, (1, len(chunk) * capacity * page), 1)
        seen = lane < 0
        for n, (r, far, i) in enumerate(chunk):
            offset, live = place(group, group ^ far, rank ^ rounds[r][i], hist_ref, owner_ref, groups, ways)
            low = (n * capacity + offset - jnp.minimum(offset, packed + 2 - capacity)) * page
            seen = seen | ((lane >= low) & (lane < low + live * page))
        masks.append(jnp.where(seen, 0.0, FLOOR).astype(jnp.float32))

    fresh, fresh_bias = None, None
    if fresh_rounds:
        fresh, shifts = refs["fresh"], [shift for shifts in fresh_rounds for shift in shifts]
        given = [ref.at[i] for shifts, ref in zip(fresh_rounds, refs["rows"]) for i in range(len(shifts))]
        units, known = fresh.shape[0], len(shifts)
        for unit in range(units):
            fresh[unit] = given[unit][...] if unit < known else jnp.zeros(fresh.shape[1:], jnp.bfloat16)
        place_of = lax.broadcasted_iota(jnp.int32, (padded, units * page), 1)
        asker = lax.broadcasted_iota(jnp.int32, (padded, units * page), 0)
        inside = remainder(place_of, page)
        token = jnp.full_like(place_of, 2 * padded)
        for unit, shift in enumerate(shifts):
            here = (place_of >= unit * page) & (place_of < (unit + 1) * page) & (inside < local_new)
            token = jnp.where(here, (rank ^ shift) * local_new + inside, token)
        if first:
            mine = lax.div(rank, ways // KVH)
            fresh[known, :, 0:HD] = refs["decode"][:, pl.ds(pl.multiple_of(mine * HD, HD), HD)]
            fresh[known, :, HD:] = refs["decode"][:, pl.ds(pl.multiple_of((KVH + mine) * HD, HD), HD)]
            here = (place_of >= known * page) & (place_of < (known + 1) * page) & (inside < decode)
            token = jnp.where(here, ways * local_new + inside, token)
        fresh_bias = jnp.where(token <= asker, 0.0, FLOOR).astype(jnp.float32)

    slope = HD ** -0.5 * math.log2(math.e)
    block_heads = min(heads, 4)
    tall = block_heads * padded

    def fold(state, query, key, value, bias):
        total, top, mixed = state
        score = lax.dot_general(query, key, (((1,), (1,)), ((), ())), preferred_element_type=jnp.float32) + bias
        new_top = jnp.maximum(top, jnp.max(score, axis=1, keepdims=True))
        weight = jnp.exp2((score - new_top) * slope)
        upper = weight.astype(jnp.bfloat16)
        lower = (weight - upper.astype(jnp.float32)).astype(jnp.bfloat16)
        wide = jnp.concatenate([value, jnp.ones_like(value)], axis=1)
        product = jnp.dot(upper, wide, preferred_element_type=jnp.float32)
        product = product + jnp.dot(lower, wide, preferred_element_type=jnp.float32)
        shrink = jnp.exp2((top - new_top) * slope)
        return total * shrink + product[:, HD:], new_top, mixed * shrink + product[:, :HD]

    blocks = dict(zip(stages[number], refs["blocks"]))
    for b in range(heads // block_heads):
        at = pl.ds(b * tall, tall)
        query = stacked[at, :].astype(jnp.bfloat16)
        if first:
            state = (jnp.zeros((tall, HD), jnp.float32), jnp.full((tall, 1), FLOOR, jnp.float32),
                     jnp.zeros((tall, HD), jnp.float32))
        else:
            both = refs["carry"][0][at, :]
            state = (both[:, HD // 2:HD // 2 + 1], both[:, :1], refs["carry"][1][at, :])
        for n, (chunk, mask) in enumerate(zip(chunks, masks)):
            def rows_of(low):
                rows_here = [blocks[r, far][i, 0:capacity, :, low:low + HD].reshape(capacity * page, HD) for r, far, i in chunk]
                if fresh is not None and n == 0:
                    rows_here.append(fresh[:, :, low:low + HD].reshape(units * page, HD))
                return jnp.concatenate(rows_here, axis=0)

            bias = mask
            if fresh is not None and n == 0:
                bias = jnp.concatenate([jnp.broadcast_to(mask, (padded, mask.shape[1])), fresh_bias], axis=1)
                bias = jnp.concatenate([bias] * block_heads, axis=0)
            state = fold(state, query, rows_of(0), rows_of(HD), bias)
        if last:
            result = state[2] / state[0]
            for h in range(block_heads):
                head = b * block_heads + h
                refs["out"][:, head * HD:(head + 1) * HD] = result[h * padded:h * padded + rows, :].astype(jnp.bfloat16)
        else:
            left = lax.broadcasted_iota(jnp.int32, (tall, HD), 1) < HD // 2
            refs["next"][0][at, :] = jnp.where(left, state[1], state[0])
            refs["next"][1][at, :] = state[2]

    for chosen, home in homeward:
        @pl.when(chosen)
        def finish():
            for copy in home:
                copy.wait()


def on_device(queries, new_kv, decode_kv, pool, hist_pages, owner, block_table):
    groups, ways = lax.axis_size("grp"), lax.axis_size("tp")
    slots, page, features = pool.shape
    capacity = slots // groups
    span = groups * ways
    rows = queries.shape[1]
    heads = H // ways
    local_new = new_kv.shape[1]
    decode = decode_kv.shape[1]
    width = features // ways
    pages_in_all = groups * block_table.shape[1] // 2
    packed = min(slots, (pages_in_all + groups * (span - 1) - ways * groups * (groups - 1) // 2) // span)
    rounds = [list(reversed(range(3 * ways // 4))), list(reversed(range(3 * ways // 4, ways)))]
    stages = [
        [(0, far) for far in range(groups // 2)],
        [(0, far) for far in range(groups // 2, groups)],
        [(1, far) for far in range(groups // 2, groups)] + [(1, far) for far in range(groups // 2)]]
    params = pltpu.CompilerParams(vmem_limit_bytes=LIMIT)
    cheap = pl.CostEstimate(flops=0, bytes_accessed=0, transcendentals=0)

    new_rows = new_kv[0]
    if local_new < page:
        new_rows = jnp.pad(new_rows, ((0, page - local_new), (0, 0)))
    decode_rows = jnp.pad(decode_kv[0], ((0, page - decode), (0, 0)))

    unit = (page, 2 * HD)
    cut = pl.pallas_call(
        functools.partial(pack_kernel, (groups, ways, capacity, packed, page, width)),
        out_shape=[jax.ShapeDtypeStruct((packed + 2,) + unit, jnp.bfloat16)] * ways,
        in_specs=[SMEM, SMEM, SMEM, ANY, VMEM],
        out_specs=[VMEM] * ways,
        scratch_shapes=[pltpu.VMEM((packed, page, features), jnp.bfloat16), pltpu.SemaphoreType.DMA((packed,))],
        compiler_params=pltpu.CompilerParams(vmem_limit_bytes=56 * 1024 * 1024),
        cost_estimate=cheap,
    )(hist_pages, owner, block_table, pool, new_rows)
    cut = list(cut)
    part = jax.ShapeDtypeStruct((packed + 2,) + unit, jnp.bfloat16)
    cut[0], cut[1] = pl.pallas_call(
        hold_kernel, out_shape=[part, part], in_specs=[VMEM, ANY], out_specs=[VMEM, ANY],
        input_output_aliases={1: 1}, compiler_params=params)(cut[0], cut[1])

    def along_tp(shift):
        return lax.ppermute(cut[shift], "tp", [(i, i ^ shift) for i in range(ways)])

    arrived = {0: cut[0]}

    def sort(shifts, before):
        sent = pl.pallas_call(
            functools.partial(regroup_kernel, (groups, ways, capacity, packed), shifts),
            out_shape=[jax.ShapeDtypeStruct((len(shifts), capacity + 1) + unit, jnp.bfloat16)] * groups + [
                jax.ShapeDtypeStruct((len(shifts),) + unit, jnp.bfloat16)],
            in_specs=[SMEM, SMEM] + [VMEM] * len(shifts) + [ANY] * len(before),
            out_specs=[VMEM] * (groups + 1),
            compiler_params=params,
            cost_estimate=cheap,
        )(hist_pages, owner, *[arrived[shift] for shift in shifts], *before)
        got = {far: lax.ppermute(sent[far], "grp", [(i, i ^ far) for i in range(groups)])
               for far in reversed(range(1, groups))}
        return [sent[0]] + [got[far] for far in range(1, groups)], sent[groups]

    tall = heads * (-(-rows // 8) * 8)
    def attend(number, carry):
        stage = stages[number]
        first, last = number == 0, number == len(stages) - 1
        args = dict(hist=hist_pages, owner=owner, query=queries[0], blocks=[parts[r][far] for r, far in stage])
        specs = dict(hist=SMEM, owner=SMEM, query=VMEM, blocks=[VMEM] * len(stage))
        scratch = dict(stacked=pltpu.VMEM((tall, HD), jnp.float32))
        if first:
            args["decode"], specs["decode"] = decode_rows, VMEM
        if carry is not None:
            args["carry"], specs["carry"] = list(carry), [VMEM] * 2
        if number < 2:
            args["rows"] = list(fresh_rows) if first else fresh_rows[-1:]
            specs["rows"] = [VMEM] * len(args["rows"])
            some = sum(array.shape[0] for array in args["rows"])
            scratch["fresh"] = pltpu.VMEM((-(-(some + 1) // 8) * 8,) + unit, jnp.bfloat16)
        if last:
            args["parts"], specs["parts"] = parts, [[ANY] * groups for unused in rounds]
            outs = dict(out=jax.ShapeDtypeStruct((rows, heads * HD), jnp.bfloat16),
                        returned=jax.ShapeDtypeStruct((ways,) + unit, jnp.bfloat16))
            out_specs = dict(out=VMEM, returned=VMEM)
            scratch["home"] = pltpu.SemaphoreType.DMA((ways,))
        else:
            outs = dict(next=[jax.ShapeDtypeStruct((tall, HD), jnp.float32)] * 2)
            out_specs = dict(next=[VMEM] * 2)
        flat_args, in_tree = jax.tree.flatten(args)
        flat_outs, out_tree = jax.tree.flatten(outs)
        flat_scratch, scratch_tree = jax.tree.flatten(scratch)

        def kernel(*flat, in_tree=in_tree, out_tree=out_tree, scratch_tree=scratch_tree, number=number):
            n, m = in_tree.num_leaves, out_tree.num_leaves
            refs = dict(jax.tree.unflatten(in_tree, flat[:n]))
            refs.update(jax.tree.unflatten(out_tree, flat[n:n + m]))
            refs.update(jax.tree.unflatten(scratch_tree, flat[n + m:]))
            dims = (groups, ways, capacity, packed, page, rows, heads, local_new, decode)
            attend_kernel(dims, refs, rounds, stages, number)

        flat = pl.pallas_call(
            kernel,
            out_shape=flat_outs,
            in_specs=jax.tree.leaves(specs),
            out_specs=jax.tree.leaves(out_specs),
            scratch_shapes=flat_scratch,
            compiler_params=params,
            cost_estimate=cheap,
        )(*flat_args)
        result = jax.tree.unflatten(out_tree, flat)
        return result

    parts, fresh_rows, result = [], [], None
    for shifts in rounds:
        arrived.update({shift: along_tp(shift) for shift in sorted(shifts) if shift})
        if shifts == rounds[-1]:
            result = attend(0, None)
        sorted_pages, sorted_rows = sort(shifts, [] if result is None else [result["next"][0]])
        parts.append(sorted_pages)
        fresh_rows.append(sorted_rows)
    for number in range(1, len(stages)):
        result = attend(number, result["next"])
    returned = result["returned"][:, :local_new, :width].reshape(1, ways * local_new, width)
    return result["out"][None], returned


def solution(mesh):
    return jax.shard_map(
        on_device,
        mesh=mesh,
        in_specs=(
            P("grp", None, "tp"),
            P("grp", "tp", None),
            P("grp", None, None),
            P(("grp", "tp"), None, None),
            P(),
            P(),
            P(),
        ),
        out_specs=(P("grp", None, "tp"), P("grp", None, "tp")),
        check_vma=False,
    )
```

```python
import functools
import math

import jax
import jax.numpy as jnp
from jax import lax
from jax.experimental import pallas as pl
from jax.experimental.pallas import tpu as pltpu
from jax.sharding import PartitionSpec as P

H = 64
KVH = 8
HD = 128
FLOOR = -1e30
ANY = pl.BlockSpec(memory_space=pl.ANY)
SMEM = pl.BlockSpec(memory_space=pltpu.SMEM)
VMEM = pl.BlockSpec(memory_space=pltpu.VMEM)
LIMIT = 32 * 1024 * 1024


def divide(value, by):
    if by & (by - 1):
        return lax.div(value, by)
    return lax.shift_right_logical(value, by.bit_length() - 1)


def remainder(value, by):
    if by & (by - 1):
        return lax.rem(value, by)
    return value & (by - 1)


def live_pages(session, group, rank, hist_ref, owner_ref, groups, ways):
    step = groups * ways
    first = remainder(group - owner_ref[session] + groups, groups) * ways + rank
    return divide(hist_ref[session] - first + step - 1, step)


def place(session, group, rank, hist_ref, owner_ref, groups, ways):
    def add(s, total):
        n = live_pages(s, group, rank, hist_ref, owner_ref, groups, ways)
        return total + jnp.where(s < session, n, 0)

    offset = lax.fori_loop(0, groups, add, jnp.int32(0), unroll=groups <= 4)
    return offset, live_pages(session, group, rank, hist_ref, owner_ref, groups, ways)


def pack_kernel(dims, hist_ref, owner_ref, table_ref, pool_ref, new_ref, *refs):
    groups, ways, capacity, packed, page, width = dims
    outs, stage, sem = refs[:ways], refs[ways], refs[ways + 1]
    group, rank = lax.axis_index("grp"), lax.axis_index("tp")
    def each_session(s, at):
        first = remainder(group - owner_ref[s] + groups, groups) * ways + rank
        count = live_pages(s, group, rank, hist_ref, owner_ref, groups, ways)

        def each_page(j, at):
            slot = table_ref[s, j * groups * ways + first]
            pltpu.make_async_copy(pool_ref.at[slot], stage.at[at], sem.at[at]).start()
            return at + 1

        return lax.fori_loop(0, count, each_page, at)

    total = lax.fori_loop(0, groups, each_session, jnp.int32(0))
    repeat = ways // KVH

    def halves(shift):
        to = rank ^ shift
        key = pl.multiple_of(lax.div(to, repeat) * HD, HD)
        value = pl.multiple_of((KVH + lax.div(to, repeat)) * HD, HD)
        return to, key, value

    for shift in range(ways):
        to, key, value = halves(shift)
        outs[shift][packed, :, 0:HD] = new_ref[:, pl.ds(key, HD)]
        outs[shift][packed, :, HD:] = new_ref[:, pl.ds(value, HD)]
        columns = pl.multiple_of(to * width, width)
        outs[shift][packed + 1, :, 0:width] = new_ref[:, pl.ds(columns, width)]

    def blank(i, unused):
        stage[i] = jnp.zeros(stage.shape[1:], stage.dtype)
        return unused

    lax.fori_loop(total, packed, blank, 0)

    def drain(i, unused):
        pltpu.make_async_copy(pool_ref.at[0], stage.at[i], sem.at[i]).wait()
        return unused

    lax.fori_loop(0, total, drain, 0)

    for shift in range(ways):
        to, key, value = halves(shift)
        outs[shift][0:packed, :, 0:HD] = stage[:, :, pl.ds(key, HD)]
        outs[shift][0:packed, :, HD:] = stage[:, :, pl.ds(value, HD)]


def hold_kernel(own_ref, other_ref, out_ref, same_ref):
    out_ref[...] = own_ref[...]


def regroup_kernel(dims, shifts, hist_ref, owner_ref, *refs):
    groups, ways, capacity, packed = dims
    count = len(shifts)
    ins, outs, fresh = refs[:count], refs[-groups - 1:-1], refs[-1]
    group, rank = lax.axis_index("grp"), lax.axis_index("tp")
    for i, shift in enumerate(shifts):
        for far in range(groups):
            offset, unused = place(group ^ far, group, rank ^ shift, hist_ref, owner_ref, groups, ways)
            start = jnp.minimum(offset, packed + 2 - capacity)
            outs[far][i, 0:capacity] = ins[i][pl.ds(start, capacity)]
            outs[far][i, capacity] = ins[i][packed + 1]
        fresh[i] = ins[i][packed]


def attend_kernel(dims, refs, rounds, stages, number):
    groups, ways, capacity, packed, page, rows, heads, local_new, decode = dims
    first, last = number == 0, number == len(stages) - 1
    fresh_rounds = rounds[:-1] if first else rounds[-1:] if number == 1 else []
    hist_ref, owner_ref, query_ref = refs["hist"], refs["owner"], refs["query"]
    padded = -(-rows // 8) * 8
    group, rank = lax.axis_index("grp"), lax.axis_index("tp")
    stacked = refs["stacked"]

    homeward = []
    if last:
        sender = jnp.int32(0)
        for s in range(groups):
            sender = sender + jnp.where(owner_ref[s] == group, s, 0)
        for far in range(groups):
            home = [pltpu.make_async_copy(
                refs["parts"][r][far].at[i, capacity], refs["returned"].at[rank ^ shift], refs["home"].at[shift])
                for r, sources in enumerate(rounds) for i, shift in enumerate(sources)]
            homeward.append(((sender ^ group) == far, home))

            @pl.when(homeward[far][0])
            def start():
                for copy in homeward[far][1]:
                    copy.start()

    stacked[...] = jnp.zeros_like(stacked)
    for head in range(heads):
        stacked[head * padded:head * padded + rows, :] = query_ref[:, head * HD:(head + 1) * HD].astype(jnp.float32)

    items = [(r, far, i) for r, far in stages[number] for i in range(len(rounds[r]))]
    many = -(-len(items) // -(-len(items) // 12))
    many = -(-many // 4) * 4
    chunks = [items[k:k + many] for k in range(0, len(items), many)]
    masks = []
    for chunk in chunks:
        lane = lax.broadcasted_iota(jnp.int32, (1, len(chunk) * capacity * page), 1)
        seen = lane < 0
        for n, (r, far, i) in enumerate(chunk):
            offset, live = place(group, group ^ far, rank ^ rounds[r][i], hist_ref, owner_ref, groups, ways)
            low = (n * capacity + offset - jnp.minimum(offset, packed + 2 - capacity)) * page
            seen = seen | ((lane >= low) & (lane < low + live * page))
        masks.append(jnp.where(seen, 0.0, FLOOR).astype(jnp.float32))

    fresh, fresh_bias = None, None
    if fresh_rounds:
        fresh, shifts = refs["fresh"], [shift for shifts in fresh_rounds for shift in shifts]
        given = [ref.at[i] for shifts, ref in zip(fresh_rounds, refs["rows"]) for i in range(len(shifts))]
        units, known = fresh.shape[0], len(shifts)
        for unit in range(units):
            fresh[unit] = given[unit][...] if unit < known else jnp.zeros(fresh.shape[1:], jnp.bfloat16)
        place_of = lax.broadcasted_iota(jnp.int32, (padded, units * page), 1)
        asker = lax.broadcasted_iota(jnp.int32, (padded, units * page), 0)
        inside = remainder(place_of, page)
        token = jnp.full_like(place_of, 2 * padded)
        for unit, shift in enumerate(shifts):
            here = (place_of >= unit * page) & (place_of < (unit + 1) * page) & (inside < local_new)
            token = jnp.where(here, (rank ^ shift) * local_new + inside, token)
        if first:
            mine = lax.div(rank, ways // KVH)
            fresh[known, :, 0:HD] = refs["decode"][:, pl.ds(pl.multiple_of(mine * HD, HD), HD)]
            fresh[known, :, HD:] = refs["decode"][:, pl.ds(pl.multiple_of((KVH + mine) * HD, HD), HD)]
            here = (place_of >= known * page) & (place_of < (known + 1) * page) & (inside < decode)
            token = jnp.where(here, ways * local_new + inside, token)
        fresh_bias = jnp.where(token <= asker, 0.0, FLOOR).astype(jnp.float32)

    slope = HD ** -0.5 * math.log2(math.e)
    block_heads = min(heads, 4)
    tall = block_heads * padded

    def fold(state, query, key, value, bias):
        total, top, mixed = state
        score = lax.dot_general(query, key, (((1,), (1,)), ((), ())), preferred_element_type=jnp.float32) + bias
        new_top = jnp.maximum(top, jnp.max(score, axis=1, keepdims=True))
        weight = jnp.exp2((score - new_top) * slope)
        upper = weight.astype(jnp.bfloat16)
        lower = (weight - upper.astype(jnp.float32)).astype(jnp.bfloat16)
        wide = jnp.concatenate([value, jnp.ones_like(value)], axis=1)
        product = jnp.dot(upper, wide, preferred_element_type=jnp.float32)
        product = product + jnp.dot(lower, wide, preferred_element_type=jnp.float32)
        shrink = jnp.exp2((top - new_top) * slope)
        return total * shrink + product[:, HD:], new_top, mixed * shrink + product[:, :HD]

    blocks = dict(zip(stages[number], refs["blocks"]))
    for b in range(heads // block_heads):
        at = pl.ds(b * tall, tall)
        query = stacked[at, :].astype(jnp.bfloat16)
        if first:
            state = (jnp.zeros((tall, HD), jnp.float32), jnp.full((tall, 1), FLOOR, jnp.float32),
                     jnp.zeros((tall, HD), jnp.float32))
        else:
            both = refs["carry"][0][at, :]
            state = (both[:, HD // 2:HD // 2 + 1], both[:, :1], refs["carry"][1][at, :])
        for n, (chunk, mask) in enumerate(zip(chunks, masks)):
            def rows_of(low):
                rows_here = [blocks[r, far][i, 0:capacity, :, low:low + HD].reshape(capacity * page, HD) for r, far, i in chunk]
                if fresh is not None and n == 0:
                    rows_here.append(fresh[:, :, low:low + HD].reshape(units * page, HD))
                return jnp.concatenate(rows_here, axis=0)

            bias = mask
            if fresh is not None and n == 0:
                bias = jnp.concatenate([jnp.broadcast_to(mask, (padded, mask.shape[1])), fresh_bias], axis=1)
                bias = jnp.concatenate([bias] * block_heads, axis=0)
            state = fold(state, query, rows_of(0), rows_of(HD), bias)
        if last:
            result = state[2] / state[0]
            for h in range(block_heads):
                head = b * block_heads + h
                refs["out"][:, head * HD:(head + 1) * HD] = result[h * padded:h * padded + rows, :].astype(jnp.bfloat16)
        else:
            left = lax.broadcasted_iota(jnp.int32, (tall, HD), 1) < HD // 2
            refs["next"][0][at, :] = jnp.where(left, state[1], state[0])
            refs["next"][1][at, :] = state[2]

    for chosen, home in homeward:
        @pl.when(chosen)
        def finish():
            for copy in home:
                copy.wait()


def on_device(queries, new_kv, decode_kv, pool, hist_pages, owner, block_table):
    groups, ways = lax.axis_size("grp"), lax.axis_size("tp")
    slots, page, features = pool.shape
    capacity = slots // groups
    span = groups * ways
    rows = queries.shape[1]
    heads = H // ways
    local_new = new_kv.shape[1]
    decode = decode_kv.shape[1]
    width = features // ways
    pages_in_all = groups * block_table.shape[1] // 2
    packed = min(slots, (pages_in_all + groups * (span - 1) - ways * groups * (groups - 1) // 2) // span)
    rounds = [list(reversed(range(3 * ways // 4))), list(reversed(range(3 * ways // 4, ways)))]
    stages = [
        [(0, far) for far in range(groups // 2)],
        [(0, far) for far in range(groups // 2, groups)],
        [(1, far) for far in range(groups // 2, groups)] + [(1, far) for far in range(groups // 2)]]
    params = pltpu.CompilerParams(vmem_limit_bytes=LIMIT)
    cheap = pl.CostEstimate(flops=0, bytes_accessed=0, transcendentals=0)

    new_rows = new_kv[0]
    if local_new < page:
        new_rows = jnp.pad(new_rows, ((0, page - local_new), (0, 0)))
    decode_rows = jnp.pad(decode_kv[0], ((0, page - decode), (0, 0)))

    unit = (page, 2 * HD)
    cut = pl.pallas_call(
        functools.partial(pack_kernel, (groups, ways, capacity, packed, page, width)),
        out_shape=[jax.ShapeDtypeStruct((packed + 2,) + unit, jnp.bfloat16)] * ways,
        in_specs=[SMEM, SMEM, SMEM, ANY, VMEM],
        out_specs=[VMEM] * ways,
        scratch_shapes=[pltpu.VMEM((packed, page, features), jnp.bfloat16), pltpu.SemaphoreType.DMA((packed,))],
        compiler_params=pltpu.CompilerParams(vmem_limit_bytes=56 * 1024 * 1024),
        cost_estimate=cheap,
    )(hist_pages, owner, block_table, pool, new_rows)
    cut = list(cut)
    part = jax.ShapeDtypeStruct((packed + 2,) + unit, jnp.bfloat16)
    cut[0], cut[1] = pl.pallas_call(
        hold_kernel, out_shape=[part, part], in_specs=[VMEM, ANY], out_specs=[VMEM, ANY],
        input_output_aliases={1: 1}, compiler_params=params)(cut[0], cut[1])

    def along_tp(shift):
        return lax.ppermute(cut[shift], "tp", [(i, i ^ shift) for i in range(ways)])

    arrived = {0: cut[0]}

    def sort(shifts, before):
        sent = pl.pallas_call(
            functools.partial(regroup_kernel, (groups, ways, capacity, packed), shifts),
            out_shape=[jax.ShapeDtypeStruct((len(shifts), capacity + 1) + unit, jnp.bfloat16)] * groups + [
                jax.ShapeDtypeStruct((len(shifts),) + unit, jnp.bfloat16)],
            in_specs=[SMEM, SMEM] + [VMEM] * len(shifts) + [ANY] * len(before),
            out_specs=[VMEM] * (groups + 1),
            compiler_params=params,
            cost_estimate=cheap,
        )(hist_pages, owner, *[arrived[shift] for shift in shifts], *before)
        got = {far: lax.ppermute(sent[far], "grp", [(i, i ^ far) for i in range(groups)])
               for far in reversed(range(1, groups))}
        return [sent[0]] + [got[far] for far in range(1, groups)], sent[groups]

    tall = heads * (-(-rows // 8) * 8)
    def attend(number, carry):
        stage = stages[number]
        first, last = number == 0, number == len(stages) - 1
        args = dict(hist=hist_pages, owner=owner, query=queries[0], blocks=[parts[r][far] for r, far in stage])
        specs = dict(hist=SMEM, owner=SMEM, query=VMEM, blocks=[VMEM] * len(stage))
        scratch = dict(stacked=pltpu.VMEM((tall + 16, HD), jnp.float32))
        if first:
            args["decode"], specs["decode"] = decode_rows, VMEM
        if carry is not None:
            args["carry"], specs["carry"] = list(carry), [VMEM] * 2
        if number < 2:
            args["rows"] = list(fresh_rows) if first else fresh_rows[-1:]
            specs["rows"] = [VMEM] * len(args["rows"])
            some = sum(array.shape[0] for array in args["rows"])
            scratch["fresh"] = pltpu.VMEM((-(-(some + 1) // 8) * 8,) + unit, jnp.bfloat16)
        if last:
            args["parts"], specs["parts"] = parts, [[ANY] * groups for unused in rounds]
            outs = dict(out=jax.ShapeDtypeStruct((rows, heads * HD), jnp.bfloat16),
                        returned=jax.ShapeDtypeStruct((ways,) + unit, jnp.bfloat16))
            out_specs = dict(out=VMEM, returned=VMEM)
            scratch["home"] = pltpu.SemaphoreType.DMA((ways,))
        else:
            outs = dict(next=[jax.ShapeDtypeStruct((tall, HD), jnp.float32)] * 2)
            out_specs = dict(next=[VMEM] * 2)
        flat_args, in_tree = jax.tree.flatten(args)
        flat_outs, out_tree = jax.tree.flatten(outs)
        flat_scratch, scratch_tree = jax.tree.flatten(scratch)

        def kernel(*flat, in_tree=in_tree, out_tree=out_tree, scratch_tree=scratch_tree, number=number):
            n, m = in_tree.num_leaves, out_tree.num_leaves
            refs = dict(jax.tree.unflatten(in_tree, flat[:n]))
            refs.update(jax.tree.unflatten(out_tree, flat[n:n + m]))
            refs.update(jax.tree.unflatten(scratch_tree, flat[n + m:]))
            dims = (groups, ways, capacity, packed, page, rows, heads, local_new, decode)
            attend_kernel(dims, refs, rounds, stages, number)

        flat = pl.pallas_call(
            kernel,
            out_shape=flat_outs,
            in_specs=jax.tree.leaves(specs),
            out_specs=jax.tree.leaves(out_specs),
            scratch_shapes=flat_scratch,
            compiler_params=params,
            cost_estimate=cheap,
        )(*flat_args)
        result = jax.tree.unflatten(out_tree, flat)
        return result

    parts, fresh_rows, result = [], [], None
    for shifts in rounds:
        arrived.update({shift: along_tp(shift) for shift in sorted(shifts) if shift})
        if shifts == rounds[-1]:
            result = attend(0, None)
        sorted_pages, sorted_rows = sort(shifts, [] if result is None else [result["next"][0]])
        parts.append(sorted_pages)
        fresh_rows.append(sorted_rows)
    for number in range(1, len(stages)):
        result = attend(number, result["next"])
    returned = result["returned"][:, :local_new, :width].reshape(1, ways * local_new, width)
    return result["out"][None], returned


def solution(mesh):
    return jax.shard_map(
        on_device,
        mesh=mesh,
        in_specs=(
            P("grp", None, "tp"),
            P("grp", "tp", None),
            P("grp", None, None),
            P(("grp", "tp"), None, None),
            P(),
            P(),
            P(),
        ),
        out_specs=(P("grp", None, "tp"), P("grp", None, "tp")),
        check_vma=False,
    )
```
